512 devices in a mesh: row: 32 (over y, x), col: 16 (over z, core).
Axes of the slice: x: 4, y: 8, z: 8, core: 2. Of those that a mesh axis runs over, the one named last changes fastest.
Arguments:
- diag_tiles: float32 [32, 256, 256], P('row'), as said below
- left_fac: bfloat16 [32, 32, 256, 128], P('row', 'col'), as said below
- right_fac: bfloat16 [32, 32, 256, 128], P('row', 'col'), as said below
- ranks: int32 [32, 32], replicated, may hold values from 16 to 128, as said below
Outputs:
- factored: float32 [32, 32, 256, 256], P('row', 'col')
The draws below stay inside these ranges and needn't reach their ends.
Inputs may be any that keep to these rules, and one draw needn't show every extreme that they name: `ranks`: every entry is a multiple of 16; in every draw some tile below the diagonal has rank 128, and the mean rank is about a third of 128. `diag_tiles`: every tile is symmetric; the first diagonal tile and the updated second diagonal tile M are positive definite. `left_fac`: entries have mean zero and deviation one. `right_fac`: entries have mean zero and deviation one over the square root of 128.
All inputs are finite; a program needn't handle non-finite values.
Results may differ from the reference program's by a relative error of at most 0.0003.
Values sent between devices are 32-bit elements; how exact they have to be, the bound alone decides.
A program may use at most 64 MiB of HBM per device.

```python
import math
import jax
import jax.numpy as jnp
from jax import lax

NT = 32
B = 256
RMAX = 128
GRID_ROWS = 32
GRID_COLS = 16


def draw_diag_tiles(key, part):
    base_key = jax.random.fold_in(key, 3)
    key_levels, key_jitter, key_links = jax.random.split(base_key, 3)
    levels = math.sqrt(B) * jnp.exp(jax.random.uniform(key_levels, (NT, B), jnp.float32, math.log(3.5), math.log(7.0)))
    jitter = 0.5 * jax.random.normal(key_jitter, (NT, B, B), jnp.float32)
    symmetric = 0.5 * (jitter + jnp.swapaxes(jitter, 1, 2))
    link_count = max(B // 4, 1)
    links = jax.random.randint(key_links, (NT, B, link_count), -2, 3).astype(jnp.int32)
    stiffness = jnp.einsum('nbk,nck->nbc', links, links).astype(jnp.float32)
    coupling = stiffness
    identity = jnp.eye(B, dtype=jnp.float32)
    return symmetric + coupling + identity[None, :, :] * levels[:, :, None]


def draw_left_fac(key, part):
    base_key = jax.random.fold_in(key, 11)
    values = jnp.clip(jax.random.normal(base_key, (NT, NT, B, RMAX), jnp.float32), -6.0, 6.0)
    return values.astype(jnp.bfloat16)


def draw_right_fac(key, part):
    base_key = jax.random.fold_in(key, 13)
    spread = 1.0 / math.sqrt(RMAX)
    values = spread * jnp.clip(jax.random.normal(base_key, (NT, NT, B, RMAX), jnp.float32), -6.0, 6.0)
    return values.astype(jnp.bfloat16)


def draw_ranks(key, part):
    base_key = jax.random.fold_in(key, 7)
    key_first, key_second, key_third, key_row, key_col = jax.random.split(base_key, 5)
    first = jax.random.randint(key_first, (NT, NT), 1, 9)
    second = jax.random.randint(key_second, (NT, NT), 1, 9)
    third = jax.random.randint(key_third, (NT, NT), 1, 9)
    levels = jnp.minimum(jnp.minimum(first, second), third)
    heavy_row = jax.random.randint(key_row, (), 1, NT)
    heavy_col = jax.random.randint(key_col, (), 0, NT) % heavy_row
    row_ids = jnp.arange(NT, dtype=jnp.int32)[:, None]
    col_ids = jnp.arange(NT, dtype=jnp.int32)[None, :]
    levels = jnp.where((row_ids == heavy_row) & (col_ids == heavy_col), 8, levels)
    return (levels * (RMAX // 8)).astype(jnp.int32)


def setup_inputs(seed: int = 0) -> dict:
    arg_keys = jax.random.split(jax.random.key(seed), 5)
    diag_tiles = draw_diag_tiles(jax.random.fold_in(arg_keys[4], 71), 0)
    left_fac = draw_left_fac(jax.random.fold_in(arg_keys[4], 71), 0)
    right_fac = draw_right_fac(jax.random.fold_in(arg_keys[4], 71), 0)
    ranks = draw_ranks(jax.random.fold_in(arg_keys[4], 71), 0)
    return dict(diag_tiles=diag_tiles, left_fac=left_fac, right_fac=right_fac, ranks=ranks)


PRECISE = lax.Precision.HIGHEST

def lower_solve(factor, stacked):
    pieces, tile_width, rank_cap = stacked.shape
    flattened = jnp.transpose(stacked, (1, 0, 2)).reshape(tile_width, pieces * rank_cap)
    solved = lax.linalg.triangular_solve(factor, flattened, left_side=True, lower=True)
    return jnp.transpose(solved.reshape(tile_width, pieces, rank_cap), (1, 0, 2))

def expand(left_basis, weights):
    return jnp.einsum('nbr,ncr->nbc', left_basis, weights, precision=PRECISE)

def reference(diag_tiles, left_fac, right_fac, ranks):
    row_slots = NT // GRID_ROWS
    col_slots = NT // GRID_COLS
    tile_index = jnp.arange(NT, dtype=jnp.int32)
    row_place = tile_index % GRID_ROWS * row_slots + tile_index // GRID_ROWS
    col_place = tile_index % GRID_COLS * col_slots + tile_index // GRID_COLS
    columns_live = jnp.arange(RMAX, dtype=jnp.int32)[None, None, :] < ranks[:, :, None]
    left_bases = jnp.where(columns_live[:, :, None, :], left_fac[row_place][:, col_place].astype(jnp.float32), 0.0)
    right_coefs = right_fac[row_place][:, col_place].astype(jnp.float32)
    diagonals = diag_tiles[row_place]
    first_pivot = jnp.linalg.cholesky(diagonals[0])
    first_basis = left_bases[:, 0]
    first_solved = lower_solve(first_pivot, right_coefs[:, 0])
    crossing = jnp.einsum('nbr,bs->nrs', first_solved, first_solved[1], precision=PRECISE)
    partial_term = jnp.matmul(first_basis[1], crossing[1], precision=PRECISE)
    shifted = diagonals[1] - jnp.matmul(partial_term, first_basis[1].T, precision=PRECISE)
    second_pivot = jnp.linalg.cholesky(shifted)
    head_basis = lax.linalg.triangular_solve(second_pivot, first_basis[1], left_side=True, lower=True)
    second_solved = lower_solve(second_pivot, right_coefs[:, 1])
    minus_term = -jnp.einsum('bs,nrs->nbr', head_basis, crossing, precision=PRECISE)
    panel_first = expand(first_basis, first_solved)
    panel_second = expand(left_bases[:, 1], second_solved) + expand(first_basis, minus_term)
    both_panels = jnp.concatenate([panel_first, panel_second], axis=2)

    def one_row(row_id):
        dense_front = jnp.einsum('jbr,jcr->jbc', left_bases[row_id], right_coefs[row_id], precision=PRECISE)
        updates = jnp.einsum('bk,jck->jbc', both_panels[row_id], both_panels, precision=PRECISE)
        schur = dense_front - updates
        col_ids = tile_index[:, None, None]
        chosen = jnp.where(col_ids == 0, panel_first[row_id][None], jnp.where(col_ids == 1, panel_second[row_id][None], schur))
        return jnp.where(col_ids < row_id, chosen, 0.0)
    natural = lax.map(one_row, tile_index)
    storage = jnp.arange(NT, dtype=jnp.int32)
    row_back = storage % row_slots * GRID_ROWS + storage // row_slots
    col_back = storage % col_slots * GRID_COLS + storage // col_slots
    return natural[row_back][:, col_back]
```

```python
import functools
import jax
import jax.numpy as jnp
from jax import lax
from jax.experimental import pallas as pl
from jax.experimental.pallas import tpu as pltpu
from jax.sharding import PartitionSpec as P

F32 = jnp.float32
MESH = pl.DeviceIdType.MESH


def across(v, k):
    return jnp.broadcast_to(v[:, k:k + 1], (8, 128))


def down(v, k):
    return jnp.broadcast_to(v[k:k + 1, :], (8, 128))


def inverse_factor(S):
    n = 16
    row = lax.broadcasted_iota(jnp.int32, (8, 128), 0)
    lane = lax.broadcasted_iota(jnp.int32, (8, 128), 1)
    R = [S[8 * i:8 * i + 8, :] for i in range(n)]
    E = [jnp.where(lane == row + 8 * i, 1.0, 0.0).astype(F32) for i in range(n)]
    out = []
    here = [across(R[0], j) for j in range(8)]
    for K in range(n):
        last = K == n - 1
        rk, ek = R[K], E[K]
        if not last:
            below = [across(R[K + 1], 8 * K + j) for j in range(8)]
            below_old = list(below)
            after = [across(R[K + 1], 8 * K + 8 + j) for j in range(8)]
        lin = jnp.zeros((8, 128), F32)
        for k in range(8):
            p = down(here[k], k)
            r = 1.0 / p
            rs = lax.rsqrt(p)
            isk = row == k
            erow = down(ek, k)
            lin = jnp.where(isk, erow * rs, lin)
            if last:
                if k < 7:
                    m = here[k] * r
                    ek = ek - m * erow
                    for j in range(k + 1, 8):
                        here[j] = here[j] - m * down(here[k], j)
                continue
            m = jnp.where(isk, 0.0, here[k] * r)
            m1 = below[k] * r
            rrow = down(rk, k)
            f = jnp.where(isk, r, 1.0)
            rk = rk * f - m * rrow
            ek = ek * f - m * erow
            for j in range(k + 1, 8):
                here[j] = here[j] * f - m * down(here[k], j)
            for j in range(8):
                after[j] = after[j] - m1 * down(below[k], j)
            for j in range(k + 1, 8):
                below[j] = below[j] - m1 * down(here[k], j)
        out.append(lin)
        if not last:
            z = [down(rk, k) for k in range(8)]
            ze = [down(ek, k) for k in range(8)]
            for I in range(K + 1, n):
                c = below_old if I == K + 1 else [across(R[I], 8 * K + j) for j in range(8)]
                a, b = R[I], E[I]
                for k in range(8):
                    a = a - c[k] * z[k]
                    b = b - c[k] * ze[k]
                R[I], E[I] = a, b
            here = after
    return jnp.concatenate(out, axis=0)


def nt(a, b):
    return lax.dot_general(a, b, (((1,), (1,)), ((), ())),
                           precision=lax.Precision.HIGHEST, preferred_element_type=F32)


def front_tile(left, right, rank):
    live = lax.broadcasted_iota(jnp.int32, left.shape, 1) < rank
    left = jnp.where(live, left.astype(F32), 0.0).astype(jnp.bfloat16)
    return lax.dot_general(left, right, (((1,), (1,)), ((), ())), preferred_element_type=F32)


class Traffic:
    def __init__(self, diag, a, d00, d11, b10, col, rowb, scratch):
        self.diag, self.a = diag, a
        self.d00, self.d11, self.b10, self.col, self.rowb = d00, d11, b10, col, rowb
        (self.d00p, self.d11p, self.b10p, self.pbuf, self.colz, self.colp, self.ss, self.rs) = scratch
        self.row = lax.axis_index("row")
        self.c = lax.axis_index("col")
        self.z = self.c // 2
        self.k = lax.rem(self.c, 2)
        self.later = []

    def remote(self, src, dst, g, **to):
        return pltpu.make_async_remote_copy(src, dst, self.ss.at[g], self.rs.at[g],
                                            device_id=to, device_id_type=MESH)

    def local(self, src, dst, g):
        pltpu.make_async_copy(src, dst, self.rs.at[g]).start()

    def arrived(self, ref, g):
        pltpu.make_async_copy(ref, ref, self.rs.at[g]).wait()

    def loop(self, n, body):
        def step(d, carry):
            body(d)
            return carry
        lax.fori_loop(1, n, step, 0)

    def run(self, cond, work):
        if cond is None:
            work(lambda copy: copy.start())
            self.later.append(lambda: work(lambda copy: copy.wait_send()))
        else:
            pl.when(cond)(lambda: work(lambda copy: copy.start()))
            self.later.append(lambda: pl.when(cond)(lambda: work(lambda copy: copy.wait_send())))

    def to_rows(self, src, dst, g, pred=None):
        def work(act):
            def one(d):
                q = lax.rem(self.row + d, 32)
                copy = self.remote(src(q), dst, g, row=q)
                if pred is None:
                    act(copy)
                else:
                    pl.when(pred(q))(lambda: act(copy))
            self.loop(32, one)
        return work

    def barrier(self):
        bar = pltpu.get_barrier_semaphore()

        def greet(**to):
            pl.semaphore_signal(bar, inc=1, device_id=to, device_id_type=MESH)
        self.loop(32, lambda d: greet(row=lax.rem(self.row + d, 32)))
        self.loop(8, lambda d: greet(col=lax.rem(self.z + d, 8) * 2 + self.k))
        greet(col=self.z * 2 + 1 - self.k)
        pl.semaphore_wait(bar, 39)

    def scatter_diag(self):
        for root, piece, g in ((0, self.d00p, 0), (1, self.d11p, 1)):
            mine = self.row == root
            self.run(mine, self.to_rows(lambda q: self.diag.at[0, pl.ds(pl.multiple_of(8 * q, 8), 8), :], piece, g))
            pl.when(mine)(functools.partial(self.local, self.diag.at[0, pl.ds(8 * root, 8), :], piece, g))

    def gather(self, piece, whole, pg, g):
        self.arrived(piece, pg)
        self.run(None, self.to_rows(lambda q: piece, whole.at[self.row], g))
        self.local(piece, whole.at[self.row], g)

    def scatter_front(self):
        a, home = self.a.at[0], self.z == 0
        self.run(home, self.to_rows(lambda q: a.at[pl.ds(pl.multiple_of(8 * q, 8), 8), :], self.pbuf.at[self.row], 2))

        def along(act):
            def one(zz):
                there = dict(col=2 * zz + self.k)
                rows = pl.ds(pl.multiple_of(32 * zz, 32), 32)
                act(self.remote(a.at[rows, :], self.rowb.at[self.k, rows, :], 3, **there))
                act(self.remote(a.at[pl.ds(0, 32), :], self.rowb.at[self.k, pl.ds(0, 32), :], 4, **there))
            self.loop(8, one)
        self.run(home, along)

        @pl.when(home)
        def _():
            self.local(a.at[pl.ds(pl.multiple_of(8 * self.row, 8), 8), :], self.pbuf.at[self.row], 2)
            self.local(a, self.rowb.at[self.k], 4)

    def front_to_planes(self):
        home = self.z == 0

        @pl.when(home)
        def _():
            self.arrived(self.pbuf, 2)

        def work(act):
            def one(zz):
                there = dict(col=2 * zz + self.k)

                @pl.when(self.k == 0)
                def _():
                    act(self.remote(self.pbuf.at[1], self.b10p, 5, **there))
                for t in range(2):
                    act(self.remote(self.pbuf.at[pl.ds(2 * zz + 16 * t, 2)], self.colz.at[t], 6, **there))
            self.loop(8, one)
        self.run(home, work)

        @pl.when(home)
        def _():
            for t in range(2):
                self.local(self.pbuf.at[pl.ds(16 * t, 2)], self.colz.at[t], 6)
            pl.when(self.k == 0)(lambda: self.local(self.pbuf.at[1], self.b10p, 5))

    def rows_along(self):
        away = self.z > 0
        mine = pl.ds(pl.multiple_of(32 * self.z, 32), 32)
        held = self.rowb.at[self.k]

        @pl.when(away)
        def _():
            self.arrived(held.at[mine, :], 3)

        def work(act):
            def one(d):
                zz = 1 + lax.rem(self.z - 1 + d, 7)
                act(self.remote(held.at[mine, :], held.at[mine, :], 4, col=2 * zz + self.k))
            self.loop(7, one)
        self.run(away, work)

    def rows_across(self):
        held = self.rowb.at[self.k]
        pl.when(self.z > 0)(lambda: self.arrived(held.at[pl.ds(0, 224), :], 4))
        pl.when(self.z == 0)(lambda: self.arrived(held, 4))
        self.run(None, lambda act: act(self.remote(held, held, 7, col=self.z * 2 + 1 - self.k)))

    def rows_done(self):
        self.arrived(self.rowb.at[1 - self.k], 7)

    def across_cores(self):
        sibling = dict(col=self.z * 2 + 1 - self.k)
        pl.when(self.k == 0)(lambda: self.arrived(self.b10p, 5))
        self.run(self.k == 0, lambda act: act(self.remote(self.b10p, self.b10p, 5, **sibling)))
        self.arrived(self.colz, 6)

        def work(act):
            for t in range(2):
                act(self.remote(self.colz.at[t, 1 - self.k], self.colp.at[t, self.k], 8, **sibling))
        self.run(None, work)
        for t in range(2):
            self.local(self.colz.at[t, self.k], self.colp.at[t, self.k], 8)

    def gather_b10(self):
        pl.when(self.k == 1)(lambda: self.arrived(self.b10p, 5))
        self.run(None, self.to_rows(lambda q: self.b10p, self.b10.at[self.row], 9))
        self.local(self.b10p, self.b10.at[self.row], 9)

    def needs(self, q, t):
        below = q > self.c + 16 * t
        return jnp.logical_and(below, self.c >= 2) if t == 0 else below

    def gather_cols(self):
        self.arrived(self.colp, 8)
        for t in range(2):
            dst = self.col.at[t, :, self.row]
            self.run(None, self.to_rows(lambda q, t=t: self.colp.at[t], dst, 12 + t, lambda q, t=t: self.needs(q, t)))
            pl.when(self.needs(self.row, t))(functools.partial(self.local, self.colp.at[t], dst, 12 + t))

    def cols_done(self):
        for t in range(2):
            pl.when(self.needs(self.row, t))(functools.partial(self.arrived, self.col.at[t], 12 + t))

    def finish(self):
        for wait in self.later:
            wait()


def own_tiles(ranks, left, right, a):
    r, c = lax.axis_index("row"), lax.axis_index("col")
    for t in range(2):
        a[t] = front_tile(left[0, t], right[0, t], ranks[r, c + 16 * t])


def whole(ref):
    return ref[...].reshape(256, 256)


def panels(d00, d11, b10, col, rowb, a, out, at):
    H = 128
    r, c = lax.axis_index("row"), lax.axis_index("col")
    at("d00")
    A = whole(d00)
    L1 = inverse_factor(A[:H, :H])
    at("one")
    T1 = nt(A[H:, :H], L1)
    L2 = inverse_factor(A[H:, H:] - nt(T1, T1))
    at("b10")
    B = whole(b10)

    def first(B):
        Fa = nt(B[:, :H], L1)
        return Fa, nt(B[:, H:] - nt(Fa, T1), L2)
    Fa, Fb = first(B)
    at("d11")
    M = whole(d11)
    L3 = inverse_factor(M[:H, :H] - nt(Fa[:H], Fa[:H]) - nt(Fb[:H], Fb[:H]))
    at("three")
    M21 = M[H:, :H] - nt(Fa[H:], Fa[:H]) - nt(Fb[H:], Fb[:H])
    T3 = nt(M21, L3)
    L4 = inverse_factor(M[H:, H:] - nt(Fa[H:], Fa[H:]) - nt(Fb[H:], Fb[H:]) - nt(T3, T3))
    at("tiles")

    def both(b0, b1):
        xa, xb = first(b0)
        C = b1 - nt(xa, Fa) - nt(xb, Fb)
        ya = nt(C[:, :H], L3)
        yb = nt(C[:, H:] - nt(ya, T3), L4)
        return [jnp.concatenate(p, axis=1) for p in ((xa, xb), (ya, yb))]
    X, Y = both(rowb[0], rowb[1])
    for t in range(2):
        j = c + 16 * t
        Xj, Yj = both(whole(col.at[t, 0]), whole(col.at[t, 1]))
        value = a[t] - nt(X, Xj) - nt(Y, Yj)
        if t == 0:
            value = jnp.where(j == 0, X, jnp.where(j == 1, Y, value))
        out[0, t] = jnp.where(j < r, value, 0.0)


def comm_scratch():
    V = pltpu.VMEM
    return [V((8, 256), F32), V((8, 256), F32), V((8, 256), F32), V((32, 8, 256), F32),
            V((2, 2, 8, 256), F32), V((2, 2, 8, 256), F32),
            pltpu.SemaphoreType.DMA((14,)), pltpu.SemaphoreType.DMA((14,))]


LAND = [(32, 8, 256), (32, 8, 256), (32, 8, 256), (2, 2, 32, 8, 256), (2, 256, 256)]


def send_kernel(ranks, diag, left, right, d00, d11, b10, col, rowb, a, *scratch):
    own_tiles(ranks, left, right, a)
    t = Traffic(diag, a, d00, d11, b10, col, rowb, scratch)
    t.barrier()
    t.scatter_diag()
    t.scatter_front()
    t.gather(t.d00p, t.d00, 0, 10)
    t.gather(t.d11p, t.d11, 1, 11)
    t.rows_along()
    t.front_to_planes()
    t.across_cores()
    t.gather_b10()
    t.gather_cols()
    t.rows_across()
    t.rows_done()
    t.arrived(t.d00, 10)
    t.arrived(t.d11, 11)
    t.arrived(t.b10, 9)
    t.cols_done()
    t.finish()


def chain_kernel(d00, d11, b10, col, rowb, a, out):
    panels(d00, d11, b10, col, rowb, a, out, lambda name: None)


def shards(diag, left, right, ranks):
    vmem = pl.BlockSpec(memory_space=pltpu.VMEM)
    landed = pl.pallas_call(
        send_kernel,
        out_shape=[jax.ShapeDtypeStruct(s, F32) for s in LAND + [(2, 256, 256)]],
        in_specs=[pl.BlockSpec(memory_space=pltpu.SMEM), pl.BlockSpec(memory_space=pl.ANY), vmem, vmem],
        out_specs=[vmem] * 6,
        scratch_shapes=comm_scratch(),
        compiler_params=pltpu.CompilerParams(collective_id=0, has_side_effects=True, vmem_limit_bytes=32 << 20),
    )(ranks, diag, left, right)
    return pl.pallas_call(
        chain_kernel,
        out_shape=jax.ShapeDtypeStruct((1, 2, 256, 256), F32),
        in_specs=[vmem] * 6,
        out_specs=vmem,
        compiler_params=pltpu.CompilerParams(vmem_limit_bytes=32 << 20),
    )(*landed)


def solution(mesh):
    in_specs = (P("row", None, None), P("row", "col", None, None), P("row", "col", None, None), P())
    return jax.shard_map(shards, mesh=mesh, in_specs=in_specs, out_specs=P("row", "col", None, None), check_vma=False)
```

```python
import functools
import jax
import jax.numpy as jnp
from jax import lax
from jax.experimental import pallas as pl
from jax.experimental.pallas import tpu as pltpu
from jax.sharding import PartitionSpec as P

F32 = jnp.float32
MESH = pl.DeviceIdType.MESH


def across(v, k):
    return jnp.broadcast_to(v[:, k:k + 1], (8, 128))


def down(v, k):
    return jnp.broadcast_to(v[k:k + 1, :], (8, 128))


def inverse_factor(S, at=lambda block: None):
    n = 16
    row = lax.broadcasted_iota(jnp.int32, (8, 128), 0)
    lane = lax.broadcasted_iota(jnp.int32, (8, 128), 1)
    R = [S[8 * i:8 * i + 8, :] for i in range(n)]
    E = [jnp.where(lane == row + 8 * i, 1.0, 0.0).astype(F32) for i in range(n)]
    out = []
    here = [across(R[0], j) for j in range(8)]
    for K in range(n):
        at(K)
        last = K == n - 1
        rk, ek = R[K], E[K]
        if not last:
            below = [across(R[K + 1], 8 * K + j) for j in range(8)]
            below_old = list(below)
            after = [across(R[K + 1], 8 * K + 8 + j) for j in range(8)]
        lin = jnp.zeros((8, 128), F32)
        for k in range(8):
            p = down(here[k], k)
            r = 1.0 / p
            rs = lax.rsqrt(p)
            isk = row == k
            erow = down(ek, k)
            lin = jnp.where(isk, erow * rs, lin)
            if last:
                if k < 7:
                    m = here[k] * r
                    ek = ek - m * erow
                    for j in range(k + 1, 8):
                        here[j] = here[j] - m * down(here[k], j)
                continue
            m = jnp.where(isk, 0.0, here[k] * r)
            m1 = below[k] * r
            rrow = down(rk, k)
            f = jnp.where(isk, r, 1.0)
            rk = rk * f - m * rrow
            ek = ek * f - m * erow
            for j in range(k + 1, 8):
                here[j] = here[j] * f - m * down(here[k], j)
            for j in range(8):
                after[j] = after[j] - m1 * down(below[k], j)
            for j in range(k + 1, 8):
                below[j] = below[j] - m1 * down(here[k], j)
        out.append(lin)
        if not last:
            z = [down(rk, k) for k in range(8)]
            ze = [down(ek, k) for k in range(8)]
            for I in range(K + 1, n):
                c = below_old if I == K + 1 else [across(R[I], 8 * K + j) for j in range(8)]
                a, b = R[I], E[I]
                for k in range(8):
                    a = a - c[k] * z[k]
                    b = b - c[k] * ze[k]
                R[I], E[I] = a, b
            here = after
    return jnp.concatenate(out, axis=0)


def nt(a, b):
    return lax.dot_general(a, b, (((1,), (1,)), ((), ())),
                           precision=lax.Precision.HIGHEST, preferred_element_type=F32)


def front_tile(left, right, rank):
    live = lax.broadcasted_iota(jnp.int32, left.shape, 1) < rank
    left = jnp.where(live, left.astype(F32), 0.0).astype(jnp.bfloat16)
    return lax.dot_general(left, right, (((1,), (1,)), ((), ())), preferred_element_type=F32)


class Traffic:
    def __init__(self, diag, a, bufs, sems):
        self.diag, self.a = diag, a
        (self.d00, self.dd, self.b10, self.col, self.rowb,
         self.d00p, self.ddp, self.b10p, self.pbuf, self.colz, self.colp) = bufs
        self.ss, self.rs = sems
        self.row = lax.axis_index("row")
        self.c = lax.axis_index("col")
        self.y, self.x = self.row // 4, lax.rem(self.row, 4)
        self.z, self.k = self.c // 2, lax.rem(self.c, 2)
        self.other = dict(col=self.z * 2 + 1 - self.k)
        self.later = []

    def remote(self, src, dst, g, **to):
        return pltpu.make_async_remote_copy(src, dst, self.ss.at[g], self.rs.at[g],
                                            device_id=to, device_id_type=MESH)

    def local(self, src, dst, g):
        pltpu.make_async_copy(src, dst, self.rs.at[g]).start()

    def arrived(self, ref, g):
        pltpu.make_async_copy(ref, ref, self.rs.at[g]).wait()

    def loop(self, lo, hi, body):
        def step(d, carry):
            body(d)
            return carry
        lax.fori_loop(lo, hi, step, 0)

    def run(self, cond, work):
        if cond is None:
            work(lambda copy: copy.start())
            self.later.append(lambda: work(lambda copy: copy.wait_send()))
        else:
            pl.when(cond)(lambda: work(lambda copy: copy.start()))
            self.later.append(lambda: pl.when(cond)(lambda: work(lambda copy: copy.wait_send())))

    def barrier(self):
        bar = pltpu.get_barrier_semaphore()

        def greet(**to):
            pl.semaphore_signal(bar, inc=1, device_id=to, device_id_type=MESH)
        self.loop(1, 32, lambda d: greet(row=lax.rem(self.row + d, 32)))
        self.loop(1, 8, lambda d: greet(col=lax.rem(self.z + d, 8) * 2 + self.k))
        greet(**self.other)
        pl.semaphore_wait(bar, 39)

    def scatter(self, cond, src, dst, g):
        def work(act):
            def one(d):
                q = lax.rem(self.row + d, 32)
                act(self.remote(src(8 * lax.rem(q, 4) + q // 4), dst, g, row=q))
            self.loop(1, 32, one)
        self.run(cond, work)
        pl.when(cond)(lambda: self.local(src(8 * self.x + self.y), dst, g))

    def block(self, rows, half):
        return self.diag.at[0, pl.ds(pl.multiple_of(rows, 8), 8), pl.ds(128 * half, 128)]

    def scatter_diag(self):
        self.scatter(self.row == 0, lambda g: self.block(8 * g, 0), self.d00p, 0)

    def scatter_rest(self):
        for root, k, lo, rows, half in ((0, 0, 0, 128, 1), (1, 0, 16, 0, 0), (1, 1, 0, 128, 0), (1, 1, 16, 128, 1)):
            mine = jnp.logical_and(self.row == root, self.k == k)

            def work(act, root=root, lo=lo, rows=rows, half=half):
                def one(i):
                    g = lo + i
                    q = 4 * lax.rem(g, 8) + g // 8
                    src = self.block(rows + 8 * i, half)
                    pl.when(q != root)(lambda: act(self.remote(src, self.ddp, 1, row=q)))
                self.loop(0, 16, one)
            self.run(mine, work)
            own = 8 * root - lo
            if 0 <= own < 16:
                pl.when(mine)(lambda: self.local(self.block(rows + 8 * own, half), self.ddp, 1))

    def along_y(self, piece, whole, pg, g, pred=None):
        self.arrived(piece, pg)
        dst = whole.at[self.x, self.y]

        def work(act):
            def one(d):
                y = lax.rem(self.y + d, 8)
                copy = self.remote(piece, dst, g, row=4 * y + self.x)
                if pred is None:
                    act(copy)
                else:
                    pl.when(pred(y))(lambda: act(copy))
            self.loop(1, 8, one)
        self.run(None, work)
        mine = lambda: self.local(piece, dst, g)
        mine() if pred is None else pl.when(pred(self.y))(mine)

    def along_x(self, whole, g, pred=None, line=None):
        held = whole.at[self.x]
        here = lambda: self.arrived(held, g)
        here() if line is None else pl.when(line(self.y))(here)

        def work(act):
            for d in (1, 3, 2):
                x = lax.rem(self.x + d, 4)
                copy = self.remote(held, held, g + 1, row=4 * self.y + x)
                if pred is None:
                    act(copy)
                else:
                    pl.when(pred(4 * self.y + x))(functools.partial(act, copy))
        self.run(None, work)

    def all_here(self, whole, g):
        self.arrived(whole.at[pl.ds(0, 3)], g + 1)

    def to_other_core(self, whole, g):
        self.all_here(whole.at[self.k], g)
        self.run(None, lambda act: act(self.remote(whole.at[self.k], whole.at[self.k], g + 2, **self.other)))

    def from_other_core(self, whole, g):
        self.arrived(whole.at[1 - self.k], g + 2)

    def scatter_front(self):
        a, home = self.a.at[0], self.z == 0
        self.scatter(home, lambda g: a.at[pl.ds(pl.multiple_of(8 * g, 8), 8), :], self.pbuf.at[self.row], 2)

    def scatter_rows(self):
        a, home = self.a.at[0], self.z == 0

        def along(act):
            def one(zz):
                there = dict(col=2 * zz + self.k)
                rows = pl.ds(pl.multiple_of(32 * zz, 32), 32)
                act(self.remote(a.at[rows, :], self.rowb.at[self.k, rows, :], 3, **there))
                act(self.remote(a.at[pl.ds(0, 32), :], self.rowb.at[self.k, pl.ds(0, 32), :], 4, **there))
            self.loop(1, 8, one)
        self.run(home, along)
        pl.when(home)(lambda: self.local(a, self.rowb.at[self.k], 4))

    def front_to_planes(self):
        home = self.z == 0
        pl.when(home)(lambda: self.arrived(self.pbuf, 2))

        def work(act):
            def one(zz):
                there = dict(col=2 * zz + self.k)

                @pl.when(self.k == 0)
                def _():
                    act(self.remote(self.pbuf.at[1], self.b10p, 5, **there))
                for t in range(2):
                    act(self.remote(self.pbuf.at[pl.ds(2 * zz + 16 * t, 2)], self.colz.at[t], 6, **there))
            self.loop(1, 8, one)
        self.run(home, work)

        @pl.when(home)
        def _():
            for t in range(2):
                self.local(self.pbuf.at[pl.ds(16 * t, 2)], self.colz.at[t], 6)
            pl.when(self.k == 0)(lambda: self.local(self.pbuf.at[1], self.b10p, 5))

    def rows_along(self):
        away = self.z > 0
        mine = pl.ds(pl.multiple_of(32 * self.z, 32), 32)
        held = self.rowb.at[self.k]
        pl.when(away)(lambda: self.arrived(held.at[mine, :], 3))

        def work(act):
            def one(d):
                zz = 1 + lax.rem(self.z - 1 + d, 7)
                act(self.remote(held.at[mine, :], held.at[mine, :], 4, col=2 * zz + self.k))
            self.loop(1, 7, one)
        self.run(away, work)

    def rows_across(self):
        held = self.rowb.at[self.k]
        pl.when(self.z > 0)(lambda: self.arrived(held.at[pl.ds(0, 224), :], 4))
        pl.when(self.z == 0)(lambda: self.arrived(held, 4))
        self.run(None, lambda act: act(self.remote(held, held, 7, **self.other)))

    def rows_done(self):
        self.arrived(self.rowb.at[1 - self.k], 7)

    def b10_to_other_core(self):
        pl.when(self.k == 0)(lambda: self.arrived(self.b10p, 5))
        self.run(self.k == 0, lambda act: act(self.remote(self.b10p, self.b10p, 5, **self.other)))

    def cols_to_other_core(self):
        self.arrived(self.colz, 6)

        def work(act):
            for t in range(2):
                act(self.remote(self.colz.at[t, 1 - self.k], self.colp.at[t, self.k], 8, **self.other))
        self.run(None, work)
        for t in range(2):
            self.local(self.colz.at[t, self.k], self.colp.at[t, self.k], 8)

    def b10_along_y(self):
        pl.when(self.k == 1)(lambda: self.arrived(self.b10p, 5))
        half = self.b10p.at[:, pl.ds(pl.multiple_of(128 * self.k, 128), 128)]
        dst = self.b10.at[self.k, self.x, self.y]
        self.run(None, lambda act: self.loop(1, 8, lambda d: act(
            self.remote(half, dst, 9, row=4 * lax.rem(self.y + d, 8) + self.x))))
        self.local(half, dst, 9)

    def needs(self, q, t):
        below = q > self.c + 16 * t
        return jnp.logical_and(below, self.c >= 2) if t == 0 else below

    def line_needs(self, y, t):
        return self.needs(4 * y + 3, t)

    def cols_along_y(self):
        self.arrived(self.colp, 8)
        for t in range(2):
            piece, dst, g = self.colp.at[t], self.col.at[t, self.x, self.y], 12 + 2 * t

            def work(act, t=t, piece=piece, dst=dst, g=g):
                def one(d):
                    y = lax.rem(self.y + d, 8)
                    pl.when(self.line_needs(y, t))(lambda: act(self.remote(piece, dst, g, row=4 * y + self.x)))
                self.loop(1, 8, one)
            self.run(None, work)
            pl.when(self.line_needs(self.y, t))(functools.partial(self.local, piece, dst, g))

    def cols_along_x(self):
        for t in range(2):
            self.along_x(self.col.at[t], 12 + 2 * t, functools.partial(self.needs, t=t),
                         functools.partial(self.line_needs, t=t))

    def cols_done(self):
        for t in range(2):
            pl.when(self.needs(self.row, t))(functools.partial(self.all_here, self.col.at[t], 12 + 2 * t))

    def finish(self):
        for wait in self.later:
            wait()


def own_tiles(ranks, left, right, a):
    r, c = lax.axis_index("row"), lax.axis_index("col")
    for t in range(2):
        a[t] = front_tile(left[0, t], right[0, t], ranks[r, c + 16 * t])


def panels(net, out, at):
    H = 128
    r, c = lax.axis_index("row"), lax.axis_index("col")
    a = net.a

    def place(name):
        return lambda block: at(name, block)
    at("d00", 0)
    A = net.d00[...].reshape(256, H)
    L1 = inverse_factor(A[:H], place("first"))
    at("a22", 0)
    U0 = net.dd[0].reshape(256, H)
    T1 = nt(A[H:], L1)
    L2 = inverse_factor(U0[:H] - nt(T1, T1), place("second"))
    at("b10", 0)
    B0, B1 = net.b10[0].reshape(256, H), net.b10[1].reshape(256, H)

    def first(B0, B1):
        Fa = nt(B0, L1)
        return Fa, nt(B1 - nt(Fa, T1), L2)
    Fa, Fb = first(B0, B1)
    U1 = net.dd[1].reshape(256, H)
    L3 = inverse_factor(U0[H:] - nt(Fa[:H], Fa[:H]) - nt(Fb[:H], Fb[:H]), place("third"))
    M21 = U1[:H] - nt(Fa[H:], Fa[:H]) - nt(Fb[H:], Fb[:H])
    T3 = nt(M21, L3)
    L4 = inverse_factor(U1[H:] - nt(Fa[H:], Fa[H:]) - nt(Fb[H:], Fb[H:]) - nt(T3, T3), place("fourth"))
    at("tiles", 0)

    def both(b0, b1):
        xa, xb = first(b0[:, :H], b0[:, H:])
        C = b1 - nt(xa, Fa) - nt(xb, Fb)
        ya = nt(C[:, :H], L3)
        yb = nt(C[:, H:] - nt(ya, T3), L4)
        return [jnp.concatenate(p, axis=1) for p in ((xa, xb), (ya, yb))]
    X, Y = both(net.rowb[0], net.rowb[1])
    for t in range(2):
        j = c + 16 * t
        Xj, Yj = both(net.col[t, :, :, 0].reshape(256, 256), net.col[t, :, :, 1].reshape(256, 256))
        value = a[t] - nt(X, Xj) - nt(Y, Yj)
        if t == 0:
            value = jnp.where(j == 0, X, jnp.where(j == 1, Y, value))
        out[0, t] = jnp.where(j < r, value, 0.0)


LAND = [(4, 8, 8, 128), (2, 4, 8, 8, 128), (2, 4, 8, 8, 128), (2, 4, 8, 2, 8, 256), (2, 256, 256)]
PIECES = [(8, 128), (8, 128), (8, 256), (32, 8, 256), (2, 2, 8, 256), (2, 2, 8, 256)]


def kernel(ranks, diag, left_hbm, right_hbm, out, left, right, a, *scratch):
    bufs, (ss, rs, ls) = scratch[:11], scratch[11:]
    loads = [pltpu.make_async_copy(left_hbm, left, ls.at[0]), pltpu.make_async_copy(right_hbm, right, ls.at[1])]
    for load in loads:
        load.start()
    t = Traffic(diag, a, bufs, (ss, rs))
    t.barrier()
    t.scatter_diag()
    for load in loads:
        load.wait()
    own_tiles(ranks, left, right, a)
    t.scatter_rest()
    t.along_y(t.d00p, t.d00, 0, 16)
    t.scatter_front()
    t.along_x(t.d00, 16)
    t.scatter_rows()
    t.along_y(t.ddp, t.dd.at[t.k], 1, 18)
    stages = {
        ("d00", 0): [lambda: t.all_here(t.d00, 16)],
        ("first", 6): [lambda: t.along_x(t.dd.at[t.k], 18), t.rows_along],
        ("first", 11): [t.front_to_planes, lambda: t.to_other_core(t.dd, 18)],
        ("a22", 0): [lambda: t.from_other_core(t.dd, 18)],
        ("second", 3): [t.b10_to_other_core, t.cols_to_other_core],
        ("second", 7): [t.b10_along_y, t.cols_along_y],
        ("second", 12): [lambda: t.along_x(t.b10.at[t.k], 9)],
        ("b10", 0): [lambda: t.to_other_core(t.b10, 9), t.cols_along_x, lambda: t.from_other_core(t.b10, 9)],
        ("third", 8): [t.rows_across],
        ("tiles", 0): [t.rows_done, t.cols_done],
    }

    def at(name, block):
        for stage in stages.get((name, block), []):
            stage()
    panels(t, out, at)
    t.finish()


def shards(diag, left, right, ranks):
    hbm = pl.BlockSpec(memory_space=pl.ANY)
    V = pltpu.VMEM
    return pl.pallas_call(
        kernel,
        out_shape=jax.ShapeDtypeStruct((1, 2, 256, 256), F32),
        in_specs=[pl.BlockSpec(memory_space=pltpu.SMEM), hbm, hbm, hbm],
        out_specs=pl.BlockSpec(memory_space=pltpu.VMEM),
        scratch_shapes=[V((1, 2, 256, 128), jnp.bfloat16), V((1, 2, 256, 128), jnp.bfloat16), V((2, 256, 256), F32)]
        + [V(s, F32) for s in LAND + PIECES]
        + [pltpu.SemaphoreType.DMA((21,)), pltpu.SemaphoreType.DMA((21,)), pltpu.SemaphoreType.DMA((2,))],
        compiler_params=pltpu.CompilerParams(collective_id=0, has_side_effects=True, vmem_limit_bytes=60 << 20),
    )(ranks, diag, left, right)


def solution(mesh):
    in_specs = (P("row", None, None), P("row", "col", None, None), P("row", "col", None, None), P())
    return jax.shard_map(shards, mesh=mesh, in_specs=in_specs, out_specs=P("row", "col", None, None), check_vma=False)
```

```python
import functools
import jax
import jax.numpy as jnp
from jax import lax
from jax.experimental import pallas as pl
from jax.experimental.pallas import tpu as pltpu
from jax.sharding import PartitionSpec as P

F32 = jnp.float32
MESH = pl.DeviceIdType.MESH


def across(v, k):
    return jnp.broadcast_to(v[:, k:k + 1], (8, 128))


def down(v, k):
    return jnp.broadcast_to(v[k:k + 1, :], (8, 128))


def inverse_factor(S, at=lambda block: None):
    n = 16
    row = lax.broadcasted_iota(jnp.int32, (8, 128), 0)
    lane = lax.broadcasted_iota(jnp.int32, (8, 128), 1)
    R = [S[8 * i:8 * i + 8, :] for i in range(n)]
    E = [jnp.where(lane == row + 8 * i, 1.0, 0.0).astype(F32) for i in range(n)]
    out = []
    here = [across(R[0], j) for j in range(8)]
    for K in range(n):
        at(K)
        last = K == n - 1
        rk, ek = R[K], E[K]
        if not last:
            below = [across(R[K + 1], 8 * K + j) for j in range(8)]
            below_old = list(below)
            after = [across(R[K + 1], 8 * K + 8 + j) for j in range(8)]
        lin = jnp.zeros((8, 128), F32)
        for k in range(8):
            p = down(here[k], k)
            r = 1.0 / p
            rs = lax.rsqrt(p)
            isk = row == k
            erow = down(ek, k)
            lin = jnp.where(isk, erow * rs, lin)
            if last:
                if k < 7:
                    m = here[k] * r
                    ek = ek - m * erow
                    for j in range(k + 1, 8):
                        here[j] = here[j] - m * down(here[k], j)
                continue
            m = jnp.where(isk, 0.0, here[k] * r)
            m1 = below[k] * r
            rrow = down(rk, k)
            f = jnp.where(isk, r, 1.0)
            rk = rk * f - m * rrow
            ek = ek * f - m * erow
            for j in range(k + 1, 8):
                here[j] = here[j] * f - m * down(here[k], j)
            for j in range(8):
                after[j] = after[j] - m1 * down(below[k], j)
            for j in range(k + 1, 8):
                below[j] = below[j] - m1 * down(here[k], j)
        out.append(lin)
        if not last:
            z = [down(rk, k) for k in range(8)]
            ze = [down(ek, k) for k in range(8)]
            for I in range(K + 1, n):
                c = below_old if I == K + 1 else [across(R[I], 8 * K + j) for j in range(8)]
                a, b = R[I], E[I]
                for k in range(8):
                    a = a - c[k] * z[k]
                    b = b - c[k] * ze[k]
                R[I], E[I] = a, b
            here = after
    return jnp.concatenate(out, axis=0)


def nt(a, b):
    return lax.dot_general(a, b, (((1,), (1,)), ((), ())),
                           precision=lax.Precision.HIGHEST, preferred_element_type=F32)


def two(v):
    high = v.astype(jnp.bfloat16)
    return high, (v - high.astype(F32)).astype(jnp.bfloat16)


def nt3(a, b):
    def one(p, q):
        return lax.dot_general(p, q, (((1,), (1,)), ((), ())), preferred_element_type=F32)
    return one(a[0], b[0]) + (one(a[0], b[1]) + one(a[1], b[0]))


def front_tile(left, right, rank):
    live = lax.broadcasted_iota(jnp.int32, left.shape, 1) < rank
    left = jnp.where(live, left.astype(F32), 0.0).astype(jnp.bfloat16)
    return lax.dot_general(left, right, (((1,), (1,)), ((), ())), preferred_element_type=F32)


class Traffic:
    def __init__(self, diag, a, bufs, sems):
        self.diag, self.a = diag, a
        (self.d00, self.dd, self.b10, self.col, self.rowb,
         self.d00p, self.ddp, self.b10p, self.colp) = bufs
        self.ss, self.rs = sems
        self.row = lax.axis_index("row")
        self.c = lax.axis_index("col")
        self.y, self.x = self.row // 4, lax.rem(self.row, 4)
        self.z, self.k = self.c // 2, lax.rem(self.c, 2)
        self.other = dict(col=self.z * 2 + 1 - self.k)
        self.later = []

    def remote(self, src, dst, g, **to):
        return pltpu.make_async_remote_copy(src, dst, self.ss.at[g], self.rs.at[g],
                                            device_id=to, device_id_type=MESH)

    def local(self, src, dst, g):
        pltpu.make_async_copy(src, dst, self.rs.at[g]).start()

    def arrived(self, ref, g):
        pltpu.make_async_copy(ref, ref, self.rs.at[g]).wait()

    def loop(self, lo, hi, body):
        def step(d, carry):
            body(d)
            return carry
        lax.fori_loop(lo, hi, step, 0)

    def run(self, cond, work):
        if cond is None:
            work(lambda copy: copy.start())
            self.later.append(lambda: work(lambda copy: copy.wait_send()))
        else:
            pl.when(cond)(lambda: work(lambda copy: copy.start()))
            self.later.append(lambda: pl.when(cond)(lambda: work(lambda copy: copy.wait_send())))

    def greet(self):
        bar = pltpu.get_barrier_semaphore()

        def tell(**to):
            pl.semaphore_signal(bar, inc=1, device_id=to, device_id_type=MESH)
        self.loop(1, 32, lambda d: tell(row=lax.rem(self.row + d, 32)))
        self.loop(1, 8, lambda d: tell(col=lax.rem(self.z + d, 8) * 2 + self.k))
        tell(**self.other)
        for t in range(2):
            source = self.c + 16 * t
            for k in range(2):
                me = jnp.logical_and(source == self.row, self.c == k)
                pl.when(jnp.logical_and(source >= 2, jnp.logical_not(me)))(
                    functools.partial(tell, row=source, col=jnp.int32(k)))

    def barrier(self):
        targets = 32 - (lax.rem(self.row, 16) == self.c).astype(jnp.int32)
        extra = jnp.where(jnp.logical_and(self.z == 0, self.row >= 2), targets, 0)
        pl.semaphore_wait(pltpu.get_barrier_semaphore(), 39 + extra)

    def from_afar(self, i):
        def swing(j, half):
            return half + (j + 1) // 2 * (1 - 2 * lax.rem(j, 2))
        y = lax.rem(self.y + swing(i // 4, 4), 8)
        x = lax.rem(self.x + swing(lax.rem(i, 4), 2), 4)
        return y, x

    def scatter(self, cond, src, dst, g):
        def work(act):
            def one(i):
                y, x = self.from_afar(i)
                act(self.remote(src(8 * x + y), dst, g, row=4 * y + x))
            self.loop(0, 31, one)
        self.run(cond, work)
        pl.when(cond)(lambda: self.local(src(8 * self.x + self.y), dst, g))

    def block(self, rows, half):
        return self.diag.at[0, pl.ds(pl.multiple_of(rows, 8), 8), pl.ds(128 * half, 128)]

    def scatter_diag(self):
        self.scatter(self.row == 0, lambda g: self.block(8 * g, 0), self.d00p, 0)

    def scatter_rest(self):
        for root, k, lo, rows, half in ((0, 0, 0, 128, 1), (1, 0, 16, 0, 0), (1, 1, 0, 128, 0), (1, 1, 16, 128, 1)):
            mine = jnp.logical_and(self.row == root, self.k == k)

            def work(act, root=root, lo=lo, rows=rows, half=half):
                def one(i):
                    g = lo + i
                    q = 4 * lax.rem(g, 8) + g // 8
                    src = self.block(rows + 8 * i, half)
                    pl.when(q != root)(lambda: act(self.remote(src, self.ddp, 1, row=q)))
                self.loop(0, 16, one)
            self.run(mine, work)
            own = 8 * root - lo
            if 0 <= own < 16:
                pl.when(mine)(lambda: self.local(self.block(rows + 8 * own, half), self.ddp, 1))

    def along_y(self, piece, whole, pg, g, pred=None):
        self.arrived(piece, pg)
        dst = whole.at[self.x, self.y]

        def work(act):
            def one(d):
                y = lax.rem(self.y + d, 8)
                copy = self.remote(piece, dst, g, row=4 * y + self.x)
                if pred is None:
                    act(copy)
                else:
                    pl.when(pred(y))(lambda: act(copy))
            self.loop(1, 8, one)
        self.run(None, work)
        mine = lambda: self.local(piece, dst, g)
        mine() if pred is None else pl.when(pred(self.y))(mine)

    def along_x(self, whole, g, pred=None, line=None):
        held = whole.at[self.x]
        here = lambda: self.arrived(held, g)
        here() if line is None else pl.when(line(self.y))(here)

        def work(act):
            for d in (1, 3, 2):
                x = lax.rem(self.x + d, 4)
                copy = self.remote(held, held, g + 1, row=4 * self.y + x)
                if pred is None:
                    act(copy)
                else:
                    pl.when(pred(4 * self.y + x))(functools.partial(act, copy))
        self.run(None, work)

    def all_here(self, whole, g):
        self.arrived(whole.at[pl.ds(0, 3)], g + 1)

    def to_other_core(self, whole, g):
        self.all_here(whole.at[self.k], g)
        self.run(None, lambda act: act(self.remote(whole.at[self.k], whole.at[self.k], g + 2, **self.other)))

    def from_other_core(self, whole, g):
        self.arrived(whole.at[1 - self.k], g + 2)

    def tile_piece(self, g):
        return self.a.at[0, pl.ds(pl.multiple_of(8 * g, 8), 8), :]

    def scatter_b10(self):
        self.scatter(jnp.logical_and(self.row == 1, self.c == 0), self.tile_piece, self.b10p, 5)

    def scatter_cols(self):
        to, t = lax.rem(self.row, 16), self.row // 16
        dst = self.colp.at[t, self.k]
        for s, g in ((0, 2), (1, 8)):
            sends = jnp.logical_and(jnp.logical_and(self.z == 0, self.row >= 2), t == s)

            def work(act, g=g):
                def one(i):
                    y, x = self.from_afar(i)
                    copy = self.remote(self.tile_piece(8 * x + y), dst, g, row=4 * y + x, col=to)
                    pl.when(jnp.logical_or(i < 31, to != self.c))(lambda: act(copy))
                self.loop(0, 32, one)
            self.run(sends, work)
            pl.when(jnp.logical_and(sends, to == self.c))(
                functools.partial(self.local, self.tile_piece(8 * self.x + self.y), dst, g))

    def scatter_rows(self):
        a, home = self.a.at[0], self.z == 0

        def along(act):
            def one(zz):
                there = dict(col=2 * zz + self.k)
                rows = pl.ds(pl.multiple_of(32 * zz, 32), 32)
                act(self.remote(a.at[rows, :], self.rowb.at[self.k, rows, :], 3, **there))
                act(self.remote(a.at[pl.ds(0, 32), :], self.rowb.at[self.k, pl.ds(0, 32), :], 4, **there))
            self.loop(1, 8, one)
        self.run(home, along)
        pl.when(home)(lambda: self.local(a, self.rowb.at[self.k], 4))

    def b10_to_planes(self):
        home = self.c == 0
        pl.when(home)(lambda: self.arrived(self.b10p, 5))
        self.run(home, lambda act: self.loop(1, 8, lambda zz: act(
            self.remote(self.b10p, self.b10p, 5, col=2 * zz + self.k))))

    def rows_along(self):
        away = self.z > 0
        mine = pl.ds(pl.multiple_of(32 * self.z, 32), 32)
        held = self.rowb.at[self.k]
        pl.when(away)(lambda: self.arrived(held.at[mine, :], 3))

        def work(act):
            def one(d):
                zz = 1 + lax.rem(self.z - 1 + d, 7)
                act(self.remote(held.at[mine, :], held.at[mine, :], 4, col=2 * zz + self.k))
            self.loop(1, 7, one)
        self.run(away, work)

    def rows_across(self):
        held = self.rowb.at[self.k]
        pl.when(self.z > 0)(lambda: self.arrived(held.at[pl.ds(0, 224), :], 4))
        pl.when(self.z == 0)(lambda: self.arrived(held, 4))
        self.run(None, lambda act: act(self.remote(held, held, 7, **self.other)))

    def rows_done(self):
        self.arrived(self.rowb.at[1 - self.k], 7)

    def b10_to_other_core(self):
        pl.when(jnp.logical_and(self.k == 0, self.z > 0))(lambda: self.arrived(self.b10p, 5))
        self.run(self.k == 0, lambda act: act(self.remote(self.b10p, self.b10p, 5, **self.other)))

    def b10_along_y(self):
        pl.when(self.k == 1)(lambda: self.arrived(self.b10p, 5))
        half = self.b10p.at[:, pl.ds(pl.multiple_of(128 * self.k, 128), 128)]
        dst = self.b10.at[self.k, self.x, self.y]
        self.run(None, lambda act: self.loop(1, 8, lambda d: act(
            self.remote(half, dst, 9, row=4 * lax.rem(self.y + d, 8) + self.x))))
        self.local(half, dst, 9)

    def needs(self, q, t):
        below = q > self.c + 16 * t
        return jnp.logical_and(below, self.c >= 2) if t == 0 else below

    def line_needs(self, y, t):
        return self.needs(4 * y + 3, t)

    def cols_along_y(self):
        for t in range(2):
            there = (lambda t=t: self.arrived(self.colp.at[t], (2, 8)[t]))
            pl.when(self.c >= 2)(there) if t == 0 else there()
            piece, dst, g = self.colp.at[t], self.col.at[t, self.x, self.y], 12 + 2 * t

            def work(act, t=t, piece=piece, dst=dst, g=g):
                def one(d):
                    y = lax.rem(self.y + d, 8)
                    pl.when(self.line_needs(y, t))(lambda: act(self.remote(piece, dst, g, row=4 * y + self.x)))
                self.loop(1, 8, one)
            self.run(None, work)
            pl.when(self.line_needs(self.y, t))(functools.partial(self.local, piece, dst, g))

    def cols_along_x(self):
        for t in range(2):
            self.along_x(self.col.at[t], 12 + 2 * t, functools.partial(self.needs, t=t),
                         functools.partial(self.line_needs, t=t))

    def cols_done(self):
        for t in range(2):
            pl.when(self.needs(self.row, t))(functools.partial(self.all_here, self.col.at[t], 12 + 2 * t))

    def finish(self):
        for wait in self.later:
            wait()


def own_tiles(ranks, left, right, a):
    r, c = lax.axis_index("row"), lax.axis_index("col")
    for t in range(2):
        a[t] = front_tile(left[0, t], right[0, t], ranks[r, c + 16 * t])


def panels(net, out, stages):
    H = 128
    r, c = lax.axis_index("row"), lax.axis_index("col")
    a = net.a
    done = {}

    def at(name, block=0):
        for stage in stages.get((name, block), []):
            stage()
        for work in works.get((name, block), []):
            work()

    def place(name):
        return lambda block: at(name, block)

    def pieces(v):
        return v[:, :H], v[:, H:]

    def row_first():
        xa, xb = first(*pieces(net.rowb[0]))
        done["X"] = [two(xa), two(xb)]

    def row_cross():
        done["C"] = cross(net.rowb[1], done["X"])

    def row_half():
        done["Y"] = half(done["C"])

    def first(b0, b1):
        fa = nt3(two(b0), done["L1"])
        fb = nt3(two(b1 - nt3(two(fa), done["T1"])), done["L2"])
        return fa, fb

    def cross(b, X):
        return b - nt3(X[0], done["Fa"]) - nt3(X[1], done["Fb"])

    def half(C):
        ya = nt3(two(C[:, :H]), done["L3"])
        return ya, C[:, H:] - nt3(two(ya), done["T3"])

    works = {("third", 6): [row_first], ("third", 10): [row_cross], ("fourth", 2): [row_half]}

    at("d00")
    A = net.d00[...].reshape(256, H)
    L1 = inverse_factor(A[:H], place("first"))
    at("a22")
    U0 = net.dd[0].reshape(256, H)
    T1 = nt(A[H:], L1)
    L2 = inverse_factor(U0[:H] - nt(T1, T1), place("second"))
    done["L1"], done["T1"], done["L2"] = two(L1), two(T1), two(L2)
    at("b10")
    B0, B1 = net.b10[0].reshape(256, H), net.b10[1].reshape(256, H)
    Fa = nt(B0, L1)
    Fb = nt(B1 - nt(Fa, T1), L2)
    done["Fa"], done["Fb"] = two(Fa), two(Fb)
    U1 = net.dd[1].reshape(256, H)
    L3 = inverse_factor(U0[H:] - nt(Fa[:H], Fa[:H]) - nt(Fb[:H], Fb[:H]), place("third"))
    M21 = U1[:H] - nt(Fa[H:], Fa[:H]) - nt(Fb[H:], Fb[:H])
    T3 = nt(M21, L3)
    done["L3"], done["T3"] = two(L3), two(T3)
    L4 = inverse_factor(U1[H:] - nt(Fa[H:], Fa[H:]) - nt(Fb[H:], Fb[H:]) - nt(T3, T3), place("fourth"))
    L4 = two(L4)
    at("tiles")
    X = done["X"]
    ya, w = done["Y"]
    yb = nt3(two(w), L4)
    rows = X + [two(ya), two(yb)]
    for t in range(2):
        j = c + 16 * t
        xa, xb = first(*pieces(net.col[t, :, :, 0].reshape(256, 256)))
        Xj = [two(xa), two(xb)]
        ja, jw = half(cross(net.col[t, :, :, 1].reshape(256, 256), Xj))
        jb = nt3(two(jw), L4)
        value = a[t]
        for left, right in zip(rows, Xj + [two(ja), two(jb)]):
            value = value - nt3(left, right)
        if t == 0:
            full = [sum(p.astype(F32) for p in v) for v in X] + [ya, yb]
            value = jnp.where(j == 0, jnp.concatenate(full[:2], axis=1),
                              jnp.where(j == 1, jnp.concatenate(full[2:], axis=1), value))
        out[0, t] = jnp.where(j < r, value, 0.0)


LAND = [(4, 8, 8, 128), (2, 4, 8, 8, 128), (2, 4, 8, 8, 128), (2, 4, 8, 2, 8, 256), (2, 256, 256)]
PIECES = [(8, 128), (8, 128), (8, 256), (2, 2, 8, 256)]


def kernel(ranks, diag, left_hbm, right_hbm, out, left, right, a, *scratch):
    bufs, (ss, rs, ls) = scratch[:9], scratch[9:]
    loads = [pltpu.make_async_copy(left_hbm, left, ls.at[0]), pltpu.make_async_copy(right_hbm, right, ls.at[1])]
    for load in loads:
        load.start()
    t = Traffic(diag, a, bufs, (ss, rs))
    t.greet()
    for load in loads:
        load.wait()
    own_tiles(ranks, left, right, a)
    t.barrier()
    t.scatter_diag()
    t.scatter_b10()
    t.scatter_rest()
    t.scatter_cols()
    t.scatter_rows()
    t.along_y(t.d00p, t.d00, 0, 16)
    t.b10_to_planes()
    t.along_y(t.ddp, t.dd.at[t.k], 1, 18)
    t.along_x(t.d00, 16)
    t.b10_to_other_core()
    t.rows_along()
    t.cols_along_y()
    t.b10_along_y()
    stages = {
        ("d00", 0): [lambda: t.all_here(t.d00, 16), lambda: t.along_x(t.dd.at[t.k], 18)],
        ("first", 12): [lambda: t.to_other_core(t.dd, 18)],
        ("a22", 0): [lambda: t.along_x(t.b10.at[t.k], 9), lambda: t.from_other_core(t.dd, 18)],
        ("second", 5): [t.cols_along_x],
        ("second", 12): [lambda: t.to_other_core(t.b10, 9)],
        ("b10", 0): [lambda: t.from_other_core(t.b10, 9)],
        ("third", 1): [t.rows_across],
        ("third", 6): [t.rows_done],
        ("tiles", 0): [t.cols_done],
    }
    panels(t, out, stages)
    t.finish()


def shards(diag, left, right, ranks):
    hbm = pl.BlockSpec(memory_space=pl.ANY)
    V = pltpu.VMEM
    return pl.pallas_call(
        kernel,
        out_shape=jax.ShapeDtypeStruct((1, 2, 256, 256), F32),
        in_specs=[pl.BlockSpec(memory_space=pltpu.SMEM), hbm, hbm, hbm],
        out_specs=pl.BlockSpec(memory_space=pltpu.VMEM),
        scratch_shapes=[V((1, 2, 256, 128), jnp.bfloat16), V((1, 2, 256, 128), jnp.bfloat16), V((2, 256, 256), F32)]
        + [V(s, F32) for s in LAND + PIECES]
        + [pltpu.SemaphoreType.DMA((21,)), pltpu.SemaphoreType.DMA((21,)), pltpu.SemaphoreType.DMA((2,))],
        compiler_params=pltpu.CompilerParams(collective_id=0, has_side_effects=True, vmem_limit_bytes=60 << 20),
    )(ranks, diag, left, right)


def solution(mesh):
    in_specs = (P("row", None, None), P("row", "col", None, None), P("row", "col", None, None), P())
    return jax.shard_map(shards, mesh=mesh, in_specs=in_specs, out_specs=P("row", "col", None, None), check_vma=False)
```

```python
import functools
import jax
import jax.numpy as jnp
from jax import lax
from jax.experimental import pallas as pl
from jax.experimental.pallas import tpu as pltpu
from jax.sharding import PartitionSpec as P

F32 = jnp.float32
MESH = pl.DeviceIdType.MESH


def across(v, k):
    return jnp.broadcast_to(v[:, k:k + 1], (8, 128))


def down(v, k):
    return jnp.broadcast_to(v[k:k + 1, :], (8, 128))


def inverse_factor(S, at=lambda block: None):
    n = 16
    row = lax.broadcasted_iota(jnp.int32, (8, 128), 0)
    lane = lax.broadcasted_iota(jnp.int32, (8, 128), 1)
    R = [S[8 * i:8 * i + 8, :] for i in range(n)]
    E = [jnp.where(lane == row + 8 * i, 1.0, 0.0).astype(F32) for i in range(n)]
    out = []
    here = [across(R[0], j) for j in range(8)]
    for K in range(n):
        at(K)
        last = K == n - 1
        rk, ek = R[K], E[K]
        if not last:
            below = [across(R[K + 1], 8 * K + j) for j in range(8)]
            below_old = list(below)
            after = [across(R[K + 1], 8 * K + 8 + j) for j in range(8)]
        lin = jnp.zeros((8, 128), F32)
        for k in range(8):
            p = down(here[k], k)
            r = 1.0 / p
            rs = lax.rsqrt(p)
            isk = row == k
            erow = down(ek, k)
            lin = jnp.where(isk, erow * rs, lin)
            if last:
                if k < 7:
                    m = here[k] * r
                    ek = ek - m * erow
                    for j in range(k + 1, 8):
                        here[j] = here[j] - m * down(here[k], j)
                continue
            m = jnp.where(isk, 0.0, here[k] * r)
            m1 = below[k] * r
            rrow = down(rk, k)
            f = jnp.where(isk, r, 1.0)
            rk = rk * f - m * rrow
            ek = ek * f - m * erow
            for j in range(k + 1, 8):
                here[j] = here[j] * f - m * down(here[k], j)
            for j in range(8):
                after[j] = after[j] - m1 * down(below[k], j)
            for j in range(k + 1, 8):
                below[j] = below[j] - m1 * down(here[k], j)
        out.append(lin)
        if not last:
            z = [down(rk, k) for k in range(8)]
            ze = [down(ek, k) for k in range(8)]
            for I in range(K + 1, n):
                c = below_old if I == K + 1 else [across(R[I], 8 * K + j) for j in range(8)]
                a, b = R[I], E[I]
                for k in range(8):
                    a = a - c[k] * z[k]
                    b = b - c[k] * ze[k]
                R[I], E[I] = a, b
            here = after
    return jnp.concatenate(out, axis=0)


def nt(a, b):
    return lax.dot_general(a, b, (((1,), (1,)), ((), ())),
                           precision=lax.Precision.HIGHEST, preferred_element_type=F32)


def two(v):
    high = v.astype(jnp.bfloat16)
    return high, (v - high.astype(F32)).astype(jnp.bfloat16)


def nt3(a, b):
    def one(p, q):
        return lax.dot_general(p, q, (((1,), (1,)), ((), ())), preferred_element_type=F32)
    return one(a[0], b[0]) + (one(a[0], b[1]) + one(a[1], b[0]))


def front_tile(left, right, rank):
    live = lax.broadcasted_iota(jnp.int32, left.shape, 1) < rank
    left = jnp.where(live, left.astype(F32), 0.0).astype(jnp.bfloat16)
    return lax.dot_general(left, right, (((1,), (1,)), ((), ())), preferred_element_type=F32)


class Traffic:
    def __init__(self, diag, a, bufs, sems):
        self.diag, self.a = diag, a
        (self.d00, self.dd, self.b10, self.col, self.rowb,
         self.d00p, self.ddp, self.b10z, self.b10p, self.colp) = bufs
        self.ss, self.rs = sems
        self.row = lax.axis_index("row")
        self.c = lax.axis_index("col")
        self.y, self.x = self.row // 4, lax.rem(self.row, 4)
        self.z, self.k = self.c // 2, lax.rem(self.c, 2)
        self.other = dict(col=self.z * 2 + 1 - self.k)
        self.later = []

    def remote(self, src, dst, g, **to):
        return pltpu.make_async_remote_copy(src, dst, self.ss.at[g], self.rs.at[g],
                                            device_id=to, device_id_type=MESH)

    def local(self, src, dst, g):
        pltpu.make_async_copy(src, dst, self.rs.at[g]).start()

    def arrived(self, ref, g):
        pltpu.make_async_copy(ref, ref, self.rs.at[g]).wait()

    def loop(self, lo, hi, body):
        def step(d, carry):
            body(d)
            return carry
        lax.fori_loop(lo, hi, step, 0)

    def run(self, cond, work, g, rows, lanes=128, times=None):
        ref = self.rowb.at[0, pl.ds(0, rows), pl.ds(0, lanes)]

        def wait():
            def one(_=0):
                pltpu.make_async_copy(ref, ref, self.ss.at[g]).wait()
            one() if times is None else self.loop(0, times, one)

        if cond is None:
            work(lambda copy: copy.start())
            self.later.append(wait)
        else:
            pl.when(cond)(lambda: work(lambda copy: copy.start()))
            self.later.append(lambda: pl.when(cond)(wait))

    def greet(self):
        bar = pltpu.get_barrier_semaphore()

        def tell(**to):
            pl.semaphore_signal(bar, inc=1, device_id=to, device_id_type=MESH)
        self.loop(1, 8, lambda d: tell(row=4 * lax.rem(self.y + d, 8) + self.x))
        self.loop(1, 4, lambda d: tell(row=4 * self.y + lax.rem(self.x + d, 4)))
        self.loop(1, 8, lambda d: tell(col=lax.rem(self.z + d, 8) * 2 + self.k))
        tell(**self.other)
        pl.when(self.k == 1)(lambda: tell(col=jnp.int32(0)))
        for root in range(2):
            pl.when(self.row != root)(functools.partial(tell, row=jnp.int32(root)))
        for t in range(2):
            source = self.c + 16 * t
            for k in range(2):
                me = jnp.logical_and(source == self.row, self.c == k)
                pl.when(jnp.logical_and(source >= 2, jnp.logical_not(me)))(
                    functools.partial(tell, row=source, col=jnp.int32(k)))

    def barrier(self):
        targets = 32 - (lax.rem(self.row, 16) == self.c).astype(jnp.int32)
        extra = jnp.where(jnp.logical_and(self.z == 0, self.row >= 2), targets, 0)
        extra = extra + jnp.where(self.row < 2, 31, 0) + jnp.where(self.c == 0, 8, 0)
        pl.semaphore_wait(pltpu.get_barrier_semaphore(), 18 + extra)

    def from_afar(self, i):
        def swing(j, half):
            return half + (j + 1) // 2 * (1 - 2 * lax.rem(j, 2))
        y = lax.rem(self.y + swing(i // 4, 4), 8)
        x = lax.rem(self.x + swing(lax.rem(i, 4), 2), 4)
        return y, x

    def scatter(self, cond, src, dst, g, lanes):
        def work(act):
            def one(i):
                y, x = self.from_afar(i)
                act(self.remote(src(8 * x + y), dst, g, row=4 * y + x))
            self.loop(0, 31, one)
        self.run(cond, work, g, 248, lanes)
        pl.when(cond)(lambda: self.local(src(8 * self.x + self.y), dst, g))

    def block(self, rows, half):
        return self.diag.at[0, pl.ds(pl.multiple_of(rows, 8), 8), pl.ds(128 * half, 128)]

    def scatter_diag(self):
        self.scatter(self.row == 0, lambda g: self.block(8 * g, 0), self.d00p, 0, 128)

    def scatter_rest(self):
        for root, k, lo, rows, half in ((0, 0, 0, 128, 1), (1, 0, 16, 0, 0), (1, 1, 0, 128, 0), (1, 1, 16, 128, 1)):
            mine = jnp.logical_and(self.row == root, self.k == k)

            def work(act, root=root, lo=lo, rows=rows, half=half):
                def one(i):
                    g = lo + i
                    q = 4 * lax.rem(g, 8) + g // 8
                    src = self.block(rows + 8 * i, half)
                    pl.when(q != root)(lambda: act(self.remote(src, self.ddp, 1, row=q)))
                self.loop(0, 16, one)
            own = 8 * root - lo
            self.run(mine, work, 1, 120 if 0 <= own < 16 else 128)
            if 0 <= own < 16:
                pl.when(mine)(lambda: self.local(self.block(rows + 8 * own, half), self.ddp, 1))

    def along_y(self, piece, whole, pg, g):
        self.arrived(piece, pg)
        dst = whole.at[self.x, self.y]

        def work(act):
            def one(d):
                act(self.remote(piece, dst, g, row=4 * lax.rem(self.y + d, 8) + self.x))
            self.loop(1, 8, one)
        self.run(None, work, g, 56)
        self.local(piece, dst, g)

    def along_x(self, whole, g):
        held = whole.at[self.x]
        self.arrived(held, g)

        def work(act):
            for d in (2, 1, 3):
                act(self.remote(held, held, g + 1, row=4 * self.y + lax.rem(self.x + d, 4)))
        self.run(None, work, g + 1, 192)

    def all_here(self, whole, g):
        self.arrived(whole.at[pl.ds(0, 3)], g + 1)

    def to_other_core(self, whole, g):
        self.all_here(whole.at[self.k], g)
        self.run(None, lambda act: act(self.remote(whole.at[self.k], whole.at[self.k], g + 2, **self.other)), g + 2, 256)

    def from_other_core(self, whole, g):
        self.arrived(whole.at[1 - self.k], g + 2)

    def tile_piece(self, g):
        return self.a.at[0, pl.ds(pl.multiple_of(8 * g, 8), 8), :]

    def scatter_b10(self):
        self.scatter(jnp.logical_and(self.row == 1, self.c == 0), self.tile_piece, self.b10z, 5, 256)

    def scatter_cols(self):
        to, t = lax.rem(self.row, 16), self.row // 16
        dst = self.colp.at[t, self.k]
        for s, g in ((0, 2), (1, 8)):
            sends = jnp.logical_and(jnp.logical_and(self.z == 0, self.row >= 2), t == s)

            def work(act, g=g):
                def one(i):
                    y, x = self.from_afar(i)
                    copy = self.remote(self.tile_piece(8 * x + y), dst, g, row=4 * y + x, col=to)
                    pl.when(jnp.logical_or(i < 31, to != self.c))(lambda: act(copy))
                self.loop(0, 32, one)
            here = to == self.c
            self.run(jnp.logical_and(sends, jnp.logical_not(here)), work, g, 256, 256)
            self.run(jnp.logical_and(sends, here), work, g, 248, 256)
            pl.when(jnp.logical_and(sends, to == self.c))(
                functools.partial(self.local, self.tile_piece(8 * self.x + self.y), dst, g))

    def scatter_rows(self):
        a, home = self.a.at[0], self.z == 0

        def along(act):
            def one(zz):
                there = dict(col=2 * zz + self.k)
                rows = pl.ds(pl.multiple_of(32 * zz, 32), 32)
                act(self.remote(a.at[rows, :], self.rowb.at[self.k, rows, :], 3, **there))
            self.loop(1, 8, one)
        self.run(home, along, 3, 224, 256)
        pl.when(home)(lambda: self.local(a, self.rowb.at[self.k], 4))

    def b10_to_planes(self):
        home = self.c == 0
        pl.when(home)(lambda: self.arrived(self.b10z, 5))

        def work(act):
            def one(c):
                half = self.b10z.at[:, pl.ds(pl.multiple_of(128 * lax.rem(c, 2), 128), 128)]
                act(self.remote(half, self.b10p, 6, col=c))
            self.loop(1, 16, one)
        self.run(home, work, 6, 120)
        pl.when(home)(lambda: self.local(self.b10z.at[:, pl.ds(0, 128)], self.b10p, 6))

    def rows_along(self):
        away = self.z > 0
        mine = pl.ds(pl.multiple_of(32 * self.z, 32), 32)
        held = self.rowb.at[self.k]
        pl.when(away)(lambda: self.arrived(held.at[mine, :], 3))

        def work(act):
            def one(d):
                zz = 1 + lax.rem(self.z - 1 + d, 7)
                act(self.remote(held.at[mine, :], held.at[mine, :], 4, col=2 * zz + self.k))
            self.loop(1, 7, one)
        self.run(away, work, 4, 192, 256)
        first = self.a.at[0, pl.ds(0, 32), :]
        self.run(self.z == 0, lambda act: self.loop(1, 8, lambda zz: act(
            self.remote(first, held.at[pl.ds(0, 32), :], 4, col=2 * zz + self.k))), 4, 224, 256)

    def rows_across(self):
        held = self.rowb.at[self.k]
        pl.when(self.z > 0)(lambda: self.arrived(held.at[pl.ds(0, 224), :], 4))
        pl.when(self.z == 0)(lambda: self.arrived(held, 4))
        self.run(None, lambda act: act(self.remote(held, held, 7, **self.other)), 7, 256, 256)

    def rows_done(self):
        self.arrived(self.rowb.at[1 - self.k], 7)

    def needs(self, q, t):
        below = q > self.c + 16 * t
        return jnp.logical_and(below, self.c >= 2) if t == 0 else below

    def line_needs(self, y, t):
        return self.needs(4 * y + 3, t)

    def cols_along_y(self):
        for t in range(2):
            there = (lambda t=t: self.arrived(self.colp.at[t], (2, 8)[t]))
            pl.when(self.c >= 2)(there) if t == 0 else there()
            piece, dst, g = self.colp.at[t], self.col.at[t, self.x, self.y], 12 + 2 * t

            def work(act, t=t, piece=piece, dst=dst, g=g):
                def one(d):
                    y = lax.rem(self.y + d, 8)
                    pl.when(self.line_needs(y, t))(lambda: act(self.remote(piece, dst, g, row=4 * y + self.x)))
                self.loop(1, 8, one)
            lines = sum(self.line_needs(lax.rem(self.y + d, 8), t).astype(jnp.int32) for d in range(1, 8))
            self.run(None, work, g, 16, 256, lines)
            pl.when(self.line_needs(self.y, t))(functools.partial(self.local, piece, dst, g))

    def cols_along_x(self):
        for t in range(2):
            held, g = self.col.at[t, self.x], 13 + 2 * t
            pl.when(self.line_needs(self.y, t))(functools.partial(self.arrived, held, g - 1))
            others = [4 * self.y + lax.rem(self.x + d, 4) for d in (2, 1, 3)]

            def work(act, t=t, held=held, g=g, others=others):
                for q in others:
                    pl.when(self.needs(q, t))(lambda: act(self.remote(held, held, g, row=q)))
            self.run(None, work, g, 128, 256, sum(self.needs(q, t).astype(jnp.int32) for q in others))

    def cols_done(self):
        for t in range(2):
            pl.when(self.needs(self.row, t))(functools.partial(self.all_here, self.col.at[t], 12 + 2 * t))

    def finish(self):
        for wait in self.later:
            wait()


def own_tiles(ranks, left, right, a):
    r, c = lax.axis_index("row"), lax.axis_index("col")
    for t in range(2):
        a[t] = front_tile(left[0, t], right[0, t], ranks[r, c + 16 * t])


def panels(net, out, stages):
    H = 128
    r, c = lax.axis_index("row"), lax.axis_index("col")
    a = net.a
    done = {}

    def at(name, block=0):
        for stage in stages.get((name, block), []):
            stage()
        for work in works.get((name, block), []):
            work()

    def place(name):
        return lambda block: at(name, block)

    def row_first():
        done["X"] = two(first(net.rowb[0]))

    def row_cross():
        done["C"] = cross(net.rowb[1], done["X"])

    def row_half():
        done["Y"] = half(done["C"])

    def first(b):
        return nt3(two(b), done["inverse"])

    def cross(b, X):
        return b - nt3(X, done["F"])

    def half(C):
        ya = nt3(two(C[:, :H]), done["L3"])
        return ya, C[:, H:] - nt3(two(ya), done["T3"])

    works = {("third", 5): [row_first], ("third", 9): [row_cross], ("fourth", 2): [row_half]}

    at("d00")
    A = net.d00[...].reshape(256, H)
    L1 = inverse_factor(A[:H], place("first"))
    at("a22")
    U0 = net.dd[0].reshape(256, H)
    T1 = nt(A[H:], L1)
    L2 = inverse_factor(U0[:H] - nt(T1, T1), place("second"))
    X1 = lax.dot(T1, L1, precision=lax.Precision.HIGHEST)
    X1 = lax.dot(L2, X1, precision=lax.Precision.HIGHEST)
    inverse = jnp.concatenate([jnp.concatenate([L1, jnp.zeros_like(L1)], axis=1),
                               jnp.concatenate([-X1, L2], axis=1)], axis=0)
    done["inverse"] = two(inverse)
    at("b10")
    F = nt(jnp.concatenate([net.b10[0].reshape(256, H), net.b10[1].reshape(256, H)], axis=1), inverse)
    done["F"] = two(F)
    U1 = net.dd[1].reshape(256, H)
    L3 = inverse_factor(U0[H:] - nt(F[:H], F[:H]), place("third"))
    M21 = U1[:H] - nt(F[H:], F[:H])
    T3 = nt(M21, L3)
    done["L3"], done["T3"] = two(L3), two(T3)
    L4 = inverse_factor(U1[H:] - nt(F[H:], F[H:]) - nt(T3, T3), place("fourth"))
    L4 = two(L4)
    at("tiles")
    X = done["X"]
    ya, w = done["Y"]
    yb = nt3(two(w), L4)
    rows = [X, two(ya), two(yb)]
    for t in range(2):
        j = c + 16 * t
        Xj = two(first(net.col[t, :, :, 0].reshape(256, 256)))
        ja, jw = half(cross(net.col[t, :, :, 1].reshape(256, 256), Xj))
        jb = nt3(two(jw), L4)
        value = a[t]
        for left, right in zip(rows, [Xj, two(ja), two(jb)]):
            value = value - nt3(left, right)
        if t == 0:
            value = jnp.where(j == 0, X[0].astype(F32) + X[1].astype(F32),
                              jnp.where(j == 1, jnp.concatenate([ya, yb], axis=1), value))
        out[0, t] = jnp.where(j < r, value, 0.0)


LAND = [(4, 8, 8, 128), (2, 4, 8, 8, 128), (2, 4, 8, 8, 128), (2, 4, 8, 2, 8, 256), (2, 256, 256)]
PIECES = [(8, 128), (8, 128), (8, 256), (8, 128), (2, 2, 8, 256)]


def kernel(ranks, diag, left_hbm, right_hbm, out, left, right, a, *scratch):
    bufs, (ss, rs, ls) = scratch[:10], scratch[10:]
    loads = [pltpu.make_async_copy(left_hbm, left, ls.at[0]), pltpu.make_async_copy(right_hbm, right, ls.at[1])]
    for load in loads:
        load.start()
    t = Traffic(diag, a, bufs, (ss, rs))
    t.greet()
    for load in loads:
        load.wait()
    own_tiles(ranks, left, right, a)
    t.barrier()
    t.scatter_b10()
    t.scatter_diag()
    t.scatter_rest()
    t.scatter_rows()
    t.scatter_cols()
    t.along_y(t.d00p, t.d00, 0, 16)
    t.b10_to_planes()
    t.along_y(t.ddp, t.dd.at[t.k], 1, 18)
    t.rows_along()
    t.along_x(t.d00, 16)
    t.along_y(t.b10p, t.b10.at[t.k], 6, 9)
    t.along_x(t.dd.at[t.k], 18)
    t.cols_along_y()
    stages = {
        ("d00", 0): [lambda: t.all_here(t.d00, 16)],
        ("a22", 0): [lambda: t.to_other_core(t.dd, 18), lambda: t.along_x(t.b10.at[t.k], 9), lambda: t.from_other_core(t.dd, 18)],
        ("b10", 0): [lambda: t.to_other_core(t.b10, 9), t.cols_along_x, lambda: t.from_other_core(t.b10, 9)],
        ("third", 1): [t.rows_across],
        ("third", 4): [t.rows_done],
        ("tiles", 0): [t.cols_done],
    }
    panels(t, out, stages)
    t.finish()


def shards(diag, left, right, ranks):
    hbm = pl.BlockSpec(memory_space=pl.ANY)
    V = pltpu.VMEM
    return pl.pallas_call(
        kernel,
        out_shape=jax.ShapeDtypeStruct((1, 2, 256, 256), F32),
        in_specs=[pl.BlockSpec(memory_space=pltpu.SMEM), hbm, hbm, hbm],
        out_specs=pl.BlockSpec(memory_space=pltpu.VMEM),
        scratch_shapes=[V((1, 2, 256, 128), jnp.bfloat16), V((1, 2, 256, 128), jnp.bfloat16), V((2, 256, 256), F32)]
        + [V(s, F32) for s in LAND + PIECES]
        + [pltpu.SemaphoreType.DMA((21,)), pltpu.SemaphoreType.DMA((21,)), pltpu.SemaphoreType.DMA((2,))],
        compiler_params=pltpu.CompilerParams(collective_id=0, has_side_effects=True, vmem_limit_bytes=60 << 20),
    )(ranks, diag, left, right)


def solution(mesh):
    in_specs = (P("row", None, None), P("row", "col", None, None), P("row", "col", None, None), P())
    return jax.shard_map(shards, mesh=mesh, in_specs=in_specs, out_specs=P("row", "col", None, None), check_vma=False)
```

```python
import functools
import jax
import jax.numpy as jnp
from jax import lax
from jax.experimental import pallas as pl
from jax.experimental.pallas import tpu as pltpu
from jax.sharding import PartitionSpec as P

F32 = jnp.float32
MESH = pl.DeviceIdType.MESH


def across(v, k):
    return jnp.broadcast_to(v[:, k:k + 1], (8, 128))


def down(v, k):
    return jnp.broadcast_to(v[k:k + 1, :], (8, 128))


def inverse_factor(S, at=lambda block: None):
    n = 16
    row = lax.broadcasted_iota(jnp.int32, (8, 128), 0)
    lane = lax.broadcasted_iota(jnp.int32, (8, 128), 1)
    R = [S[8 * i:8 * i + 8, :] for i in range(n)]
    E = [jnp.where(lane == row + 8 * i, 1.0, 0.0).astype(F32) for i in range(n)]
    out = []
    here = [across(R[0], j) for j in range(8)]
    for K in range(n):
        at(K)
        last = K == n - 1
        rk, ek = R[K], E[K]
        if not last:
            below = [across(R[K + 1], 8 * K + j) for j in range(8)]
            below_old = list(below)
            after = [across(R[K + 1], 8 * K + 8 + j) for j in range(8)]
        lin = jnp.zeros((8, 128), F32)
        for k in range(8):
            p = down(here[k], k)
            r = 1.0 / p
            rs = lax.rsqrt(p)
            isk = row == k
            erow = down(ek, k)
            lin = jnp.where(isk, erow * rs, lin)
            if last:
                if k < 7:
                    m = here[k] * r
                    ek = ek - m * erow
                    for j in range(k + 1, 8):
                        here[j] = here[j] - m * down(here[k], j)
                continue
            m = jnp.where(isk, 0.0, here[k] * r)
            m1 = below[k] * r
            rrow = down(rk, k)
            f = jnp.where(isk, r, 1.0)
            rk = rk * f - m * rrow
            ek = ek * f - m * erow
            for j in range(k + 1, 8):
                here[j] = here[j] * f - m * down(here[k], j)
            for j in range(8):
                after[j] = after[j] - m1 * down(below[k], j)
            for j in range(k + 1, 8):
                below[j] = below[j] - m1 * down(here[k], j)
        out.append(lin)
        if not last:
            z = [down(rk, k) for k in range(8)]
            ze = [down(ek, k) for k in range(8)]
            for I in range(K + 1, n):
                c = below_old if I == K + 1 else [across(R[I], 8 * K + j) for j in range(8)]
                a, b = R[I], E[I]
                for k in range(8):
                    a = a - c[k] * z[k]
                    b = b - c[k] * ze[k]
                R[I], E[I] = a, b
            here = after
    return jnp.concatenate(out, axis=0)


def parts(v):
    high = v.astype(jnp.bfloat16)
    rest = v - high.astype(F32)
    middle = rest.astype(jnp.bfloat16)
    return high, middle, (rest - middle.astype(F32)).astype(jnp.bfloat16)


def nt(a, b):
    a1, a2, a3 = parts(a)
    b1, b2, b3 = parts(b)
    return lax.dot_general(jnp.concatenate([a3, a2, a1, a2, a1, a1], axis=1),
                           jnp.concatenate([b1, b2, b3, b1, b2, b1], axis=1),
                           (((1,), (1,)), ((), ())), preferred_element_type=F32)


def two(v):
    high = v.astype(jnp.bfloat16)
    return high, (v - high.astype(F32)).astype(jnp.bfloat16)


def nt3(a, b):
    def one(p, q):
        return lax.dot_general(p, q, (((1,), (1,)), ((), ())), preferred_element_type=F32)
    return one(a[0], b[0]) + (one(a[0], b[1]) + one(a[1], b[0]))


def front_tile(left, right, rank):
    live = lax.broadcasted_iota(jnp.int32, left.shape, 1) < rank
    left = jnp.where(live, left.astype(F32), 0.0).astype(jnp.bfloat16)
    return lax.dot_general(left, right, (((1,), (1,)), ((), ())), preferred_element_type=F32)


class Traffic:
    def __init__(self, diag, a, bufs, sems):
        self.diag, self.a = diag, a
        (self.d00, self.dd, self.b10, self.col, self.rowb,
         self.d00p, self.ddp, self.b10z, self.b10p, self.colp) = bufs
        self.ss, self.rs = sems
        self.row = lax.axis_index("row")
        self.c = lax.axis_index("col")
        self.y, self.x = self.row // 4, lax.rem(self.row, 4)
        self.z, self.k = self.c // 2, lax.rem(self.c, 2)
        self.other = dict(col=self.z * 2 + 1 - self.k)
        self.later = []

    def remote(self, src, dst, g, **to):
        return pltpu.make_async_remote_copy(src, dst, self.ss.at[g], self.rs.at[g],
                                            device_id=to, device_id_type=MESH)

    def local(self, src, dst, g):
        pltpu.make_async_copy(src, dst, self.rs.at[g]).start()

    def arrived(self, ref, g):
        pltpu.make_async_copy(ref, ref, self.rs.at[g]).wait()

    def loop(self, lo, hi, body):
        def step(d, carry):
            body(d)
            return carry
        lax.fori_loop(lo, hi, step, 0)

    def run(self, cond, work, g, rows, lanes=128, times=None):
        ref = self.rowb.at[0, pl.ds(0, rows), pl.ds(0, lanes)]

        def wait():
            def one(_=0):
                pltpu.make_async_copy(ref, ref, self.ss.at[g]).wait()
            one() if times is None else self.loop(0, times, one)

        if cond is None:
            work(lambda copy: copy.start())
            self.later.append(wait)
        else:
            pl.when(cond)(lambda: work(lambda copy: copy.start()))
            self.later.append(lambda: pl.when(cond)(wait))

    def greet(self):
        bar = pltpu.get_barrier_semaphore()

        def tell(**to):
            pl.semaphore_signal(bar, inc=1, device_id=to, device_id_type=MESH)
        self.loop(1, 8, lambda d: tell(row=4 * lax.rem(self.y + d, 8) + self.x))
        self.loop(1, 4, lambda d: tell(row=4 * self.y + lax.rem(self.x + d, 4)))
        self.loop(1, 8, lambda d: tell(col=lax.rem(self.z + d, 8) * 2 + self.k))
        tell(**self.other)
        pl.when(self.k == 1)(lambda: tell(col=jnp.int32(0)))
        for root in range(2):
            pl.when(self.row != root)(functools.partial(tell, row=jnp.int32(root)))
        for t in range(2):
            source = self.c + 16 * t
            for k in range(2):
                me = jnp.logical_and(source == self.row, self.c == k)
                pl.when(jnp.logical_and(source >= 2, jnp.logical_not(me)))(
                    functools.partial(tell, row=source, col=jnp.int32(k)))

    def barrier(self):
        targets = 32 - (lax.rem(self.row, 16) == self.c).astype(jnp.int32)
        extra = jnp.where(jnp.logical_and(self.z == 0, self.row >= 2), targets, 0)
        extra = extra + jnp.where(self.row < 2, 31, 0) + jnp.where(self.c == 0, 8, 0)
        pl.semaphore_wait(pltpu.get_barrier_semaphore(), 18 + extra)

    def from_afar(self, i):
        def swing(j, half):
            return half + (j + 1) // 2 * (1 - 2 * lax.rem(j, 2))
        y = lax.rem(self.y + swing(i // 4, 4), 8)
        x = lax.rem(self.x + swing(lax.rem(i, 4), 2), 4)
        return y, x

    def scatter(self, cond, src, dst, g, lanes):
        def work(act):
            def one(i):
                y, x = self.from_afar(i)
                act(self.remote(src(8 * x + y), dst, g, row=4 * y + x))
            self.loop(0, 31, one)
        self.run(cond, work, g, 248, lanes)
        pl.when(cond)(lambda: self.local(src(8 * self.x + self.y), dst, g))

    def block(self, rows, half):
        return self.diag.at[0, pl.ds(pl.multiple_of(rows, 8), 8), pl.ds(128 * half, 128)]

    def scatter_diag(self):
        self.scatter(self.row == 0, lambda g: self.block(8 * g, 0), self.d00p, 0, 128)

    def scatter_rest(self):
        for root, k, lo, rows, half in ((0, 0, 0, 128, 1), (1, 0, 16, 0, 0), (1, 1, 0, 128, 0), (1, 1, 16, 128, 1)):
            mine = jnp.logical_and(self.row == root, self.k == k)

            def work(act, root=root, lo=lo, rows=rows, half=half):
                def one(i):
                    g = lo + i
                    q = 4 * lax.rem(g, 8) + g // 8
                    src = self.block(rows + 8 * i, half)
                    pl.when(q != root)(lambda: act(self.remote(src, self.ddp, 1, row=q)))
                self.loop(0, 16, one)
            own = 8 * root - lo
            self.run(mine, work, 1, 120 if 0 <= own < 16 else 128)
            if 0 <= own < 16:
                pl.when(mine)(lambda: self.local(self.block(rows + 8 * own, half), self.ddp, 1))

    def along_y(self, piece, whole, pg, g):
        self.arrived(piece, pg)
        dst = whole.at[self.x, self.y]

        def work(act):
            def one(d):
                act(self.remote(piece, dst, g, row=4 * lax.rem(self.y + d, 8) + self.x))
            self.loop(1, 8, one)
        self.run(None, work, g, 56)
        self.local(piece, dst, g)

    def along_x(self, whole, g):
        held = whole.at[self.x]
        self.arrived(held, g)

        def work(act):
            for d in (2, 1, 3):
                act(self.remote(held, held, g + 1, row=4 * self.y + lax.rem(self.x + d, 4)))
        self.run(None, work, g + 1, 192)

    def all_here(self, whole, g):
        self.arrived(whole.at[pl.ds(0, 3)], g + 1)

    def to_other_core(self, whole, g):
        self.all_here(whole.at[self.k], g)
        self.run(None, lambda act: act(self.remote(whole.at[self.k], whole.at[self.k], g + 2, **self.other)), g + 2, 256)

    def from_other_core(self, whole, g):
        self.arrived(whole.at[1 - self.k], g + 2)

    def tile_piece(self, g):
        return self.a.at[0, pl.ds(pl.multiple_of(8 * g, 8), 8), :]

    def scatter_b10(self):
        self.scatter(jnp.logical_and(self.row == 1, self.c == 0), self.tile_piece, self.b10z, 5, 256)

    def scatter_cols(self):
        to, t = lax.rem(self.row, 16), self.row // 16
        dst = self.colp.at[t, self.k]
        for s, g in ((0, 2), (1, 8)):
            sends = jnp.logical_and(jnp.logical_and(self.z == 0, self.row >= 2), t == s)

            def work(act, g=g):
                def one(i):
                    y, x = self.from_afar(i)
                    copy = self.remote(self.tile_piece(8 * x + y), dst, g, row=4 * y + x, col=to)
                    pl.when(jnp.logical_or(i < 31, to != self.c))(lambda: act(copy))
                self.loop(0, 32, one)
            here = to == self.c
            self.run(jnp.logical_and(sends, jnp.logical_not(here)), work, g, 256, 256)
            self.run(jnp.logical_and(sends, here), work, g, 248, 256)
            pl.when(jnp.logical_and(sends, to == self.c))(
                functools.partial(self.local, self.tile_piece(8 * self.x + self.y), dst, g))

    def scatter_rows(self):
        a, home = self.a.at[0], self.z == 0

        def along(act):
            def one(zz):
                there = dict(col=2 * zz + self.k)
                rows = pl.ds(pl.multiple_of(32 * zz, 32), 32)
                act(self.remote(a.at[rows, :], self.rowb.at[self.k, rows, :], 3, **there))
            self.loop(1, 8, one)
        self.run(home, along, 3, 224, 256)
        pl.when(home)(lambda: self.local(a, self.rowb.at[self.k], 4))

    def b10_to_planes(self):
        home = self.c == 0
        pl.when(home)(lambda: self.arrived(self.b10z, 5))

        def work(act):
            def one(c):
                half = self.b10z.at[:, pl.ds(pl.multiple_of(128 * lax.rem(c, 2), 128), 128)]
                act(self.remote(half, self.b10p, 6, col=c))
            self.loop(1, 16, one)
        self.run(home, work, 6, 120)
        pl.when(home)(lambda: self.local(self.b10z.at[:, pl.ds(0, 128)], self.b10p, 6))

    def rows_along(self):
        away = self.z > 0
        mine = pl.ds(pl.multiple_of(32 * self.z, 32), 32)
        held = self.rowb.at[self.k]
        pl.when(away)(lambda: self.arrived(held.at[mine, :], 3))

        def work(act):
            def one(d):
                zz = 1 + lax.rem(self.z - 1 + d, 7)
                act(self.remote(held.at[mine, :], held.at[mine, :], 4, col=2 * zz + self.k))
            self.loop(1, 7, one)
        self.run(away, work, 4, 192, 256)
        first = self.a.at[0, pl.ds(0, 32), :]
        self.run(self.z == 0, lambda act: self.loop(1, 8, lambda zz: act(
            self.remote(first, held.at[pl.ds(0, 32), :], 4, col=2 * zz + self.k))), 4, 224, 256)

    def rows_across(self):
        held = self.rowb.at[self.k]
        pl.when(self.z > 0)(lambda: self.arrived(held.at[pl.ds(0, 224), :], 4))
        pl.when(self.z == 0)(lambda: self.arrived(held, 4))
        self.run(None, lambda act: act(self.remote(held, held, 7, **self.other)), 7, 256, 256)

    def rows_done(self):
        self.arrived(self.rowb.at[1 - self.k], 7)

    def needs(self, q, t):
        below = q > self.c + 16 * t
        return jnp.logical_and(below, self.c >= 2) if t == 0 else below

    def line_needs(self, y, t):
        return self.needs(4 * y + 3, t)

    def cols_along_y(self):
        for t in range(2):
            there = (lambda t=t: self.arrived(self.colp.at[t], (2, 8)[t]))
            pl.when(self.c >= 2)(there) if t == 0 else there()
            piece, dst, g = self.colp.at[t], self.col.at[t, self.x, self.y], 12 + 2 * t

            def work(act, t=t, piece=piece, dst=dst, g=g):
                def one(d):
                    y = lax.rem(self.y + d, 8)
                    pl.when(self.line_needs(y, t))(lambda: act(self.remote(piece, dst, g, row=4 * y + self.x)))
                self.loop(1, 8, one)
            lines = sum(self.line_needs(lax.rem(self.y + d, 8), t).astype(jnp.int32) for d in range(1, 8))
            self.run(None, work, g, 16, 256, lines)
            pl.when(self.line_needs(self.y, t))(functools.partial(self.local, piece, dst, g))

    def cols_along_x(self):
        for t in range(2):
            held, g = self.col.at[t, self.x], 13 + 2 * t
            pl.when(self.line_needs(self.y, t))(functools.partial(self.arrived, held, g - 1))
            others = [4 * self.y + lax.rem(self.x + d, 4) for d in (2, 1, 3)]

            def work(act, t=t, held=held, g=g, others=others):
                for q in others:
                    pl.when(self.needs(q, t))(lambda: act(self.remote(held, held, g, row=q)))
            self.run(None, work, g, 128, 256, sum(self.needs(q, t).astype(jnp.int32) for q in others))

    def cols_done(self):
        for t in range(2):
            pl.when(self.needs(self.row, t))(functools.partial(self.all_here, self.col.at[t], 12 + 2 * t))

    def finish(self):
        for wait in self.later:
            wait()


def own_tiles(ranks, left, right, a):
    r, c = lax.axis_index("row"), lax.axis_index("col")
    for t in range(2):
        a[t] = front_tile(left[0, t], right[0, t], ranks[r, c + 16 * t])


def panels(net, out, stages):
    H = 128
    r, c = lax.axis_index("row"), lax.axis_index("col")
    a = net.a
    done = {}

    def at(name, block=0):
        for stage in stages.get((name, block), []):
            stage()
        for work in works.get((name, block), []):
            work()

    def place(name):
        return lambda block: at(name, block)

    def row_first():
        done["X"] = two(first(net.rowb[0]))

    def row_cross():
        done["C"] = cross(net.rowb[1], done["X"])

    def col_first(t):
        done["col", t] = two(first(net.col[t, :, :, 0].reshape(256, 256)))

    def col_half(t):
        Xj = done["col", t]
        done["tile", t] = Xj, half(cross(net.col[t, :, :, 1].reshape(256, 256), Xj))

    def row_half():
        done["Y"] = half(done["C"])

    def first(b):
        return nt3(two(b), done["inverse"])

    def cross(b, X):
        return b - nt3(X, done["F"])

    def half(C):
        ya = nt3(two(C[:, :H]), done["L3"])
        return ya, C[:, H:] - nt3(two(ya), done["T3"])

    works = {("third", 5): [row_first], ("third", 9): [row_cross], ("fourth", 2): [row_half],
             ("fourth", 10): [functools.partial(col_first, 0)], ("fourth", 11): [functools.partial(col_first, 1)],
             ("fourth", 12): [functools.partial(col_half, 0)], ("fourth", 14): [functools.partial(col_half, 1)]}

    at("d00")
    A = net.d00[...].reshape(256, H)
    L1 = inverse_factor(A[:H], place("first"))
    at("a22")
    U0 = net.dd[0].reshape(256, H)
    T1 = nt(A[H:], L1)
    L2 = inverse_factor(U0[:H] - nt(T1, T1), place("second"))
    X1 = lax.dot(T1, L1, precision=lax.Precision.HIGHEST)
    X1 = lax.dot(L2, X1, precision=lax.Precision.HIGHEST)
    inverse = jnp.concatenate([jnp.concatenate([L1, jnp.zeros_like(L1)], axis=1),
                               jnp.concatenate([-X1, L2], axis=1)], axis=0)
    done["inverse"] = two(inverse)
    at("b10")
    F = nt(jnp.concatenate([net.b10[0].reshape(256, H), net.b10[1].reshape(256, H)], axis=1), inverse)
    done["F"] = two(F)
    U1 = net.dd[1].reshape(256, H)
    L3 = inverse_factor(U0[H:] - nt(F[:H], F[:H]), place("third"))
    M21 = U1[:H] - nt(F[H:], F[:H])
    T3 = nt(M21, L3)
    done["L3"], done["T3"] = two(L3), two(T3)
    L4 = inverse_factor(U1[H:] - nt(F[H:], F[H:]) - nt(T3, T3), place("fourth"))
    L4 = two(L4)
    at("tiles")
    X = done["X"]
    ya, w = done["Y"]
    yb = nt3(two(w), L4)
    rows = [X, two(ya), two(yb)]
    for t in range(2):
        j = c + 16 * t
        Xj, (ja, jw) = done["tile", t]
        jb = nt3(two(jw), L4)
        value = a[t]
        for left, right in zip(rows, [Xj, two(ja), two(jb)]):
            value = value - nt3(left, right)
        if t == 0:
            value = jnp.where(j == 0, X[0].astype(F32) + X[1].astype(F32),
                              jnp.where(j == 1, jnp.concatenate([ya, yb], axis=1), value))
        out[0, t] = jnp.where(j < r, value, 0.0)


LAND = [(4, 8, 8, 128), (2, 4, 8, 8, 128), (2, 4, 8, 8, 128), (2, 4, 8, 2, 8, 256), (2, 256, 256)]
PIECES = [(8, 128), (8, 128), (8, 256), (8, 128), (2, 2, 8, 256)]


def kernel(ranks, diag, left_hbm, right_hbm, out, left, right, a, *scratch):
    bufs, (ss, rs, ls) = scratch[:10], scratch[10:]
    loads = [pltpu.make_async_copy(left_hbm, left, ls.at[0]), pltpu.make_async_copy(right_hbm, right, ls.at[1])]
    for load in loads:
        load.start()
    t = Traffic(diag, a, bufs, (ss, rs))
    t.greet()
    for load in loads:
        load.wait()
    own_tiles(ranks, left, right, a)
    t.barrier()
    t.scatter_b10()
    t.scatter_diag()
    t.scatter_rest()
    t.scatter_rows()
    t.scatter_cols()
    t.along_y(t.d00p, t.d00, 0, 16)
    t.b10_to_planes()
    t.along_y(t.ddp, t.dd.at[t.k], 1, 18)
    t.rows_along()
    t.along_x(t.d00, 16)
    t.along_y(t.b10p, t.b10.at[t.k], 6, 9)
    t.along_x(t.dd.at[t.k], 18)
    t.cols_along_y()
    stages = {
        ("d00", 0): [lambda: t.all_here(t.d00, 16)],
        ("a22", 0): [lambda: t.to_other_core(t.dd, 18), lambda: t.along_x(t.b10.at[t.k], 9), lambda: t.from_other_core(t.dd, 18)],
        ("b10", 0): [lambda: t.to_other_core(t.b10, 9), t.cols_along_x, lambda: t.from_other_core(t.b10, 9)],
        ("third", 1): [t.rows_across],
        ("third", 4): [t.rows_done],
        ("fourth", 9): [t.cols_done],
    }
    panels(t, out, stages)
    t.finish()


def shards(diag, left, right, ranks):
    hbm = pl.BlockSpec(memory_space=pl.ANY)
    V = pltpu.VMEM
    return pl.pallas_call(
        kernel,
        out_shape=jax.ShapeDtypeStruct((1, 2, 256, 256), F32),
        in_specs=[pl.BlockSpec(memory_space=pltpu.SMEM), hbm, hbm, hbm],
        out_specs=pl.BlockSpec(memory_space=pltpu.VMEM),
        scratch_shapes=[V((1, 2, 256, 128), jnp.bfloat16), V((1, 2, 256, 128), jnp.bfloat16), V((2, 256, 256), F32)]
        + [V(s, F32) for s in LAND + PIECES]
        + [pltpu.SemaphoreType.DMA((21,)), pltpu.SemaphoreType.DMA((21,)), pltpu.SemaphoreType.DMA((2,))],
        compiler_params=pltpu.CompilerParams(collective_id=0, has_side_effects=True, vmem_limit_bytes=60 << 20),
    )(ranks, diag, left, right)


def solution(mesh):
    in_specs = (P("row", None, None), P("row", "col", None, None), P("row", "col", None, None), P())
    return jax.shard_map(shards, mesh=mesh, in_specs=in_specs, out_specs=P("row", "col", None, None), check_vma=False)
```

```python
import functools
import jax
import jax.numpy as jnp
from jax import lax
from jax.experimental import pallas as pl
from jax.experimental.pallas import tpu as pltpu
from jax.sharding import PartitionSpec as P

F32 = jnp.float32
MESH = pl.DeviceIdType.MESH


def across(v, k):
    return jnp.broadcast_to(v[:, k:k + 1], (8, 128))


def down(v, k):
    return jnp.broadcast_to(v[k:k + 1, :], (8, 128))


def inverse_factor(S, at=lambda block: None):
    n = 16
    row = lax.broadcasted_iota(jnp.int32, (8, 128), 0)
    lane = lax.broadcasted_iota(jnp.int32, (8, 128), 1)
    R = [S[8 * i:8 * i + 8, :] for i in range(n)]
    E = [jnp.where(lane == row + 8 * i, 1.0, 0.0).astype(F32) for i in range(n)]
    out = []
    here = [across(R[0], j) for j in range(8)]
    for K in range(n):
        at(K)
        last = K == n - 1
        rk, ek = R[K], E[K]
        if not last:
            below = [across(R[K + 1], 8 * K + j) for j in range(8)]
            below_old = list(below)
            after = [across(R[K + 1], 8 * K + 8 + j) for j in range(8)]
        lin = jnp.zeros((8, 128), F32)
        for k in range(8):
            p = down(here[k], k)
            r = 1.0 / p
            rs = lax.rsqrt(p)
            isk = row == k
            erow = down(ek, k)
            lin = jnp.where(isk, erow * rs, lin)
            if last:
                if k < 7:
                    m = here[k] * r
                    ek = ek - m * erow
                    for j in range(k + 1, 8):
                        here[j] = here[j] - m * down(here[k], j)
                continue
            m = jnp.where(isk, 0.0, here[k] * r)
            m1 = below[k] * r
            rrow = down(rk, k)
            f = jnp.where(isk, r, 1.0)
            rk = rk * f - m * rrow
            ek = ek * f - m * erow
            for j in range(k + 1, 8):
                here[j] = here[j] * f - m * down(here[k], j)
            for j in range(8):
                after[j] = after[j] - m1 * down(below[k], j)
            for j in range(k + 1, 8):
                below[j] = below[j] - m1 * down(here[k], j)
        out.append(lin)
        if not last:
            z = [down(rk, k) for k in range(8)]
            ze = [down(ek, k) for k in range(8)]
            for I in range(K + 1, min(K + 5, n)):
                c = below_old if I == K + 1 else [across(R[I], 8 * K + j) for j in range(8)]
                for k in range(8):
                    R[I] = R[I] - c[k] * z[k]
                    E[I] = E[I] - c[k] * ze[k]
            if K + 5 < n:
                a1, a2, a3 = [v.astype(F32) for v in parts(R[K])]
                b1, b2, b3 = [v.astype(F32) for v in parts(jnp.concatenate([rk, ek], axis=1))]
                less = lax.dot_general(jnp.concatenate([a1, a1, a2, a1, a3, a2], axis=0).astype(jnp.bfloat16),
                                       jnp.concatenate([b1, b2, b1, b3, b1, b2], axis=0).astype(jnp.bfloat16),
                                       (((0,), (0,)), ((), ())), preferred_element_type=F32)
                for I in range(K + 5, n):
                    R[I] = R[I] - less[8 * I:8 * I + 8, :128]
                    E[I] = E[I] - less[8 * I:8 * I + 8, 128:]
            here = after
    return jnp.concatenate(out, axis=0)


def parts(v):
    high = v.astype(jnp.bfloat16)
    rest = v - high.astype(F32)
    middle = rest.astype(jnp.bfloat16)
    return high, middle, (rest - middle.astype(F32)).astype(jnp.bfloat16)


def nt(a, b):
    a1, a2, a3 = parts(a)
    b1, b2, b3 = parts(b)
    return lax.dot_general(jnp.concatenate([a3, a2, a1, a2, a1, a1], axis=1),
                           jnp.concatenate([b1, b2, b3, b1, b2, b1], axis=1),
                           (((1,), (1,)), ((), ())), preferred_element_type=F32)


def two(v):
    high = v.astype(jnp.bfloat16)
    return high, (v - high.astype(F32)).astype(jnp.bfloat16)


def nt3(a, b):
    def one(p, q):
        return lax.dot_general(p, q, (((1,), (1,)), ((), ())), preferred_element_type=F32)
    return one(a[0], b[0]) + (one(a[0], b[1]) + one(a[1], b[0]))


def front_tile(left, right, rank):
    live = lax.broadcasted_iota(jnp.int32, left.shape, 1) < rank
    left = jnp.where(live, left.astype(F32), 0.0).astype(jnp.bfloat16)
    return lax.dot_general(left, right, (((1,), (1,)), ((), ())), preferred_element_type=F32)


class Traffic:
    def __init__(self, diag, a, bufs, sems):
        self.diag, self.a = diag, a
        (self.d00, self.dd, self.b10, self.col, self.rowb,
         self.d00p, self.ddp, self.b10z, self.b10p, self.colp) = bufs
        self.ss, self.rs = sems
        self.row = lax.axis_index("row")
        self.c = lax.axis_index("col")
        self.y, self.x = self.row // 4, lax.rem(self.row, 4)
        self.z, self.k = self.c // 2, lax.rem(self.c, 2)
        self.other = dict(col=self.z * 2 + 1 - self.k)
        self.later = []

    def remote(self, src, dst, g, **to):
        return pltpu.make_async_remote_copy(src, dst, self.ss.at[g], self.rs.at[g],
                                            device_id=to, device_id_type=MESH)

    def local(self, src, dst, g):
        pltpu.make_async_copy(src, dst, self.rs.at[g]).start()

    def arrived(self, ref, g):
        pltpu.make_async_copy(ref, ref, self.rs.at[g]).wait()

    def loop(self, lo, hi, body):
        def step(d, carry):
            body(d)
            return carry
        lax.fori_loop(lo, hi, step, 0)

    def run(self, cond, work, g, rows, lanes=128, times=None):
        ref = self.rowb.at[0, pl.ds(0, rows), pl.ds(0, lanes)]

        def wait():
            def one(_=0):
                pltpu.make_async_copy(ref, ref, self.ss.at[g]).wait()
            one() if times is None else self.loop(0, times, one)

        if cond is None:
            work(lambda copy: copy.start())
            self.later.append(wait)
        else:
            pl.when(cond)(lambda: work(lambda copy: copy.start()))
            self.later.append(lambda: pl.when(cond)(wait))

    def greet(self):
        bar = pltpu.get_barrier_semaphore()

        def tell(**to):
            pl.semaphore_signal(bar, inc=1, device_id=to, device_id_type=MESH)
        self.loop(1, 8, lambda d: tell(row=4 * lax.rem(self.y + d, 8) + self.x))
        self.loop(1, 4, lambda d: tell(row=4 * self.y + lax.rem(self.x + d, 4)))
        self.loop(1, 8, lambda d: tell(col=lax.rem(self.z + d, 8) * 2 + self.k))
        tell(**self.other)
        pl.when(self.k == 1)(lambda: tell(col=jnp.int32(0)))
        for root in range(2):
            pl.when(self.row != root)(functools.partial(tell, row=jnp.int32(root)))
        for t in range(2):
            source = self.c + 16 * t
            for k in range(2):
                me = jnp.logical_and(source == self.row, self.c == k)
                pl.when(jnp.logical_and(source >= 2, jnp.logical_not(me)))(
                    functools.partial(tell, row=source, col=jnp.int32(k)))

    def barrier(self):
        targets = 32 - (lax.rem(self.row, 16) == self.c).astype(jnp.int32)
        extra = jnp.where(jnp.logical_and(self.z == 0, self.row >= 2), targets, 0)
        extra = extra + jnp.where(self.row < 2, 31, 0) + jnp.where(self.c == 0, 8, 0)
        pl.semaphore_wait(pltpu.get_barrier_semaphore(), 18 + extra)

    def from_afar(self, i):
        def swing(j, half):
            return half + (j + 1) // 2 * (1 - 2 * lax.rem(j, 2))
        y = lax.rem(self.y + swing(i // 4, 4), 8)
        x = lax.rem(self.x + swing(lax.rem(i, 4), 2), 4)
        return y, x

    def scatter(self, cond, src, dst, g, lanes):
        def work(act):
            def one(i):
                y, x = self.from_afar(i)
                act(self.remote(src(8 * x + y), dst, g, row=4 * y + x))
            self.loop(0, 31, one)
        self.run(cond, work, g, 248, lanes)
        pl.when(cond)(lambda: self.local(src(8 * self.x + self.y), dst, g))

    def block(self, rows, half):
        return self.diag.at[0, pl.ds(pl.multiple_of(rows, 8), 8), pl.ds(128 * half, 128)]

    def scatter_diag(self):
        self.scatter(self.row == 0, lambda g: self.block(8 * g, 0), self.d00p, 0, 128)

    def scatter_rest(self):
        for root, k, lo, rows, half in ((0, 0, 0, 128, 1), (1, 0, 16, 0, 0), (1, 1, 0, 128, 0), (1, 1, 16, 128, 1)):
            mine = jnp.logical_and(self.row == root, self.k == k)

            def work(act, root=root, lo=lo, rows=rows, half=half):
                def one(i):
                    g = lo + i
                    q = 4 * lax.rem(g, 8) + g // 8
                    src = self.block(rows + 8 * i, half)
                    pl.when(q != root)(lambda: act(self.remote(src, self.ddp, 1, row=q)))
                self.loop(0, 16, one)
            own = 8 * root - lo
            self.run(mine, work, 1, 120 if 0 <= own < 16 else 128)
            if 0 <= own < 16:
                pl.when(mine)(lambda: self.local(self.block(rows + 8 * own, half), self.ddp, 1))

    def along_y(self, piece, whole, pg, g):
        self.arrived(piece, pg)
        dst = whole.at[self.x, self.y]

        def work(act):
            def one(d):
                act(self.remote(piece, dst, g, row=4 * lax.rem(self.y + d, 8) + self.x))
            self.loop(1, 8, one)
        self.run(None, work, g, 56)
        self.local(piece, dst, g)

    def along_x(self, whole, g):
        held = whole.at[self.x]
        self.arrived(held, g)

        def work(act):
            for d in (2, 1, 3):
                act(self.remote(held, held, g + 1, row=4 * self.y + lax.rem(self.x + d, 4)))
        self.run(None, work, g + 1, 192)

    def all_here(self, whole, g):
        self.arrived(whole.at[pl.ds(0, 3)], g + 1)

    def to_other_core(self, whole, g):
        self.all_here(whole.at[self.k], g)
        self.run(None, lambda act: act(self.remote(whole.at[self.k], whole.at[self.k], g + 2, **self.other)), g + 2, 256)

    def from_other_core(self, whole, g):
        self.arrived(whole.at[1 - self.k], g + 2)

    def tile_piece(self, g):
        return self.a.at[0, pl.ds(pl.multiple_of(8 * g, 8), 8), :]

    def scatter_b10(self):
        self.scatter(jnp.logical_and(self.row == 1, self.c == 0), self.tile_piece, self.b10z, 5, 256)

    def scatter_cols(self):
        to, t = lax.rem(self.row, 16), self.row // 16
        dst = self.colp.at[t, self.k]
        for s, g in ((0, 2), (1, 8)):
            sends = jnp.logical_and(jnp.logical_and(self.z == 0, self.row >= 2), t == s)

            def work(act, g=g):
                def one(i):
                    y, x = self.from_afar(i)
                    copy = self.remote(self.tile_piece(8 * x + y), dst, g, row=4 * y + x, col=to)
                    pl.when(jnp.logical_or(i < 31, to != self.c))(lambda: act(copy))
                self.loop(0, 32, one)
            here = to == self.c
            self.run(jnp.logical_and(sends, jnp.logical_not(here)), work, g, 256, 256)
            self.run(jnp.logical_and(sends, here), work, g, 248, 256)
            pl.when(jnp.logical_and(sends, to == self.c))(
                functools.partial(self.local, self.tile_piece(8 * self.x + self.y), dst, g))

    def scatter_rows(self):
        a, home = self.a.at[0], self.z == 0

        def along(act):
            def one(zz):
                there = dict(col=2 * zz + self.k)
                rows = pl.ds(pl.multiple_of(32 * zz, 32), 32)
                act(self.remote(a.at[rows, :], self.rowb.at[self.k, rows, :], 3, **there))
            self.loop(1, 8, one)
        self.run(home, along, 3, 224, 256)
        pl.when(home)(lambda: self.local(a, self.rowb.at[self.k], 4))

    def b10_to_planes(self):
        home = self.c == 0
        pl.when(home)(lambda: self.arrived(self.b10z, 5))

        def work(act):
            def one(c):
                half = self.b10z.at[:, pl.ds(pl.multiple_of(128 * lax.rem(c, 2), 128), 128)]
                act(self.remote(half, self.b10p, 6, col=c))
            self.loop(1, 16, one)
        self.run(home, work, 6, 120)
        pl.when(home)(lambda: self.local(self.b10z.at[:, pl.ds(0, 128)], self.b10p, 6))

    def rows_along(self):
        away = self.z > 0
        mine = pl.ds(pl.multiple_of(32 * self.z, 32), 32)
        held = self.rowb.at[self.k]
        pl.when(away)(lambda: self.arrived(held.at[mine, :], 3))

        def work(act):
            def one(d):
                zz = 1 + lax.rem(self.z - 1 + d, 7)
                act(self.remote(held.at[mine, :], held.at[mine, :], 4, col=2 * zz + self.k))
            self.loop(1, 7, one)
        self.run(away, work, 4, 192, 256)
        first = self.a.at[0, pl.ds(0, 32), :]
        self.run(self.z == 0, lambda act: self.loop(1, 8, lambda zz: act(
            self.remote(first, held.at[pl.ds(0, 32), :], 4, col=2 * zz + self.k))), 4, 224, 256)

    def rows_across(self):
        held = self.rowb.at[self.k]
        pl.when(self.z > 0)(lambda: self.arrived(held.at[pl.ds(0, 224), :], 4))
        pl.when(self.z == 0)(lambda: self.arrived(held, 4))
        self.run(None, lambda act: act(self.remote(held, held, 7, **self.other)), 7, 256, 256)

    def rows_done(self):
        self.arrived(self.rowb.at[1 - self.k], 7)

    def needs(self, q, t):
        below = q > self.c + 16 * t
        return jnp.logical_and(below, self.c >= 2) if t == 0 else below

    def line_needs(self, y, t):
        return self.needs(4 * y + 3, t)

    def cols_along_y(self):
        for t in range(2):
            there = (lambda t=t: self.arrived(self.colp.at[t], (2, 8)[t]))
            pl.when(self.c >= 2)(there) if t == 0 else there()
            piece, dst, g = self.colp.at[t], self.col.at[t, self.x, self.y], 12 + 2 * t

            def work(act, t=t, piece=piece, dst=dst, g=g):
                def one(d):
                    y = lax.rem(self.y + d, 8)
                    pl.when(self.line_needs(y, t))(lambda: act(self.remote(piece, dst, g, row=4 * y + self.x)))
                self.loop(1, 8, one)
            lines = sum(self.line_needs(lax.rem(self.y + d, 8), t).astype(jnp.int32) for d in range(1, 8))
            self.run(None, work, g, 16, 256, lines)
            pl.when(self.line_needs(self.y, t))(functools.partial(self.local, piece, dst, g))

    def cols_along_x(self):
        for t in range(2):
            held, g = self.col.at[t, self.x], 13 + 2 * t
            pl.when(self.line_needs(self.y, t))(functools.partial(self.arrived, held, g - 1))
            others = [4 * self.y + lax.rem(self.x + d, 4) for d in (2, 1, 3)]

            def work(act, t=t, held=held, g=g, others=others):
                for q in others:
                    pl.when(self.needs(q, t))(lambda: act(self.remote(held, held, g, row=q)))
            self.run(None, work, g, 128, 256, sum(self.needs(q, t).astype(jnp.int32) for q in others))

    def cols_done(self):
        for t in range(2):
            pl.when(self.needs(self.row, t))(functools.partial(self.all_here, self.col.at[t], 12 + 2 * t))

    def finish(self):
        for wait in self.later:
            wait()


def own_tiles(ranks, left, right, a):
    r, c = lax.axis_index("row"), lax.axis_index("col")
    for t in range(2):
        a[t] = front_tile(left[0, t], right[0, t], ranks[r, c + 16 * t])


def panels(net, out, stages):
    H = 128
    r, c = lax.axis_index("row"), lax.axis_index("col")
    a = net.a
    done = {}

    def at(name, block=0):
        for stage in stages.get((name, block), []):
            stage()
        for work in works.get((name, block), []):
            work()

    def place(name):
        return lambda block: at(name, block)

    def row_first():
        done["X"] = two(first(net.rowb[0]))

    def row_cross():
        done["C"] = cross(net.rowb[1], done["X"])

    def col_first(t):
        done["col", t] = two(first(net.col[t, :, :, 0].reshape(256, 256)))

    def col_half(t):
        Xj = done["col", t]
        done["tile", t] = Xj, half(cross(net.col[t, :, :, 1].reshape(256, 256), Xj))

    def row_half():
        done["Y"] = half(done["C"])

    def first(b):
        return nt3(two(b), done["inverse"])

    def cross(b, X):
        return b - nt3(X, done["F"])

    def half(C):
        ya = nt3(two(C[:, :H]), done["L3"])
        return ya, C[:, H:] - nt3(two(ya), done["T3"])

    works = {("third", 5): [row_first], ("third", 9): [row_cross], ("fourth", 2): [row_half],
             ("fourth", 10): [functools.partial(col_first, 0)], ("fourth", 11): [functools.partial(col_first, 1)],
             ("fourth", 12): [functools.partial(col_half, 0)], ("fourth", 14): [functools.partial(col_half, 1)]}

    at("d00")
    A = net.d00[...].reshape(256, H)
    L1 = inverse_factor(A[:H], place("first"))
    at("a22")
    U0 = net.dd[0].reshape(256, H)
    T1 = nt(A[H:], L1)
    L2 = inverse_factor(U0[:H] - nt(T1, T1), place("second"))
    X1 = lax.dot(T1, L1, precision=lax.Precision.HIGHEST)
    X1 = lax.dot(L2, X1, precision=lax.Precision.HIGHEST)
    inverse = jnp.concatenate([jnp.concatenate([L1, jnp.zeros_like(L1)], axis=1),
                               jnp.concatenate([-X1, L2], axis=1)], axis=0)
    done["inverse"] = two(inverse)
    at("b10")
    F = nt(jnp.concatenate([net.b10[0].reshape(256, H), net.b10[1].reshape(256, H)], axis=1), inverse)
    done["F"] = two(F)
    U1 = net.dd[1].reshape(256, H)
    L3 = inverse_factor(U0[H:] - nt(F[:H], F[:H]), place("third"))
    M21 = U1[:H] - nt(F[H:], F[:H])
    T3 = nt(M21, L3)
    done["L3"], done["T3"] = two(L3), two(T3)
    L4 = inverse_factor(U1[H:] - nt(F[H:], F[H:]) - nt(T3, T3), place("fourth"))
    L4 = two(L4)
    at("tiles")
    X = done["X"]
    ya, w = done["Y"]
    yb = nt3(two(w), L4)
    rows = [X, two(ya), two(yb)]
    for t in range(2):
        j = c + 16 * t
        Xj, (ja, jw) = done["tile", t]
        jb = nt3(two(jw), L4)
        value = a[t]
        for left, right in zip(rows, [Xj, two(ja), two(jb)]):
            value = value - nt3(left, right)
        if t == 0:
            value = jnp.where(j == 0, X[0].astype(F32) + X[1].astype(F32),
                              jnp.where(j == 1, jnp.concatenate([ya, yb], axis=1), value))
        out[0, t] = jnp.where(j < r, value, 0.0)


LAND = [(4, 8, 8, 128), (2, 4, 8, 8, 128), (2, 4, 8, 8, 128), (2, 4, 8, 2, 8, 256), (2, 256, 256)]
PIECES = [(8, 128), (8, 128), (8, 256), (8, 128), (2, 2, 8, 256)]


def kernel(ranks, diag_hbm, left_hbm, right_hbm, out, left, right, a, diag, *scratch):
    bufs, (ss, rs, ls) = scratch[:10], scratch[10:]
    loads = [pltpu.make_async_copy(left_hbm, left, ls.at[0]), pltpu.make_async_copy(right_hbm, right, ls.at[1]),
             pltpu.make_async_copy(diag_hbm, diag, ls.at[2])]
    for load in loads:
        load.start()
    t = Traffic(diag, a, bufs, (ss, rs))
    t.greet()
    for load in loads:
        load.wait()
    own_tiles(ranks, left, right, a)
    t.barrier()
    t.scatter_b10()
    t.scatter_diag()
    t.scatter_rest()
    t.scatter_rows()
    t.scatter_cols()
    t.along_y(t.d00p, t.d00, 0, 16)
    t.b10_to_planes()
    t.along_y(t.ddp, t.dd.at[t.k], 1, 18)
    t.rows_along()
    t.along_x(t.d00, 16)
    t.along_y(t.b10p, t.b10.at[t.k], 6, 9)
    t.along_x(t.dd.at[t.k], 18)
    t.cols_along_y()
    stages = {
        ("d00", 0): [lambda: t.all_here(t.d00, 16)],
        ("a22", 0): [lambda: t.to_other_core(t.dd, 18), lambda: t.along_x(t.b10.at[t.k], 9), lambda: t.from_other_core(t.dd, 18)],
        ("second", 14): [lambda: t.to_other_core(t.b10, 9)],
        ("b10", 0): [lambda: t.from_other_core(t.b10, 9)],
        ("third", 0): [t.cols_along_x],
        ("third", 2): [t.rows_across],
        ("third", 4): [t.rows_done],
        ("fourth", 9): [t.cols_done],
    }
    panels(t, out, stages)
    t.finish()


def shards(diag, left, right, ranks):
    hbm = pl.BlockSpec(memory_space=pl.ANY)
    V = pltpu.VMEM
    return pl.pallas_call(
        kernel,
        out_shape=jax.ShapeDtypeStruct((1, 2, 256, 256), F32),
        in_specs=[pl.BlockSpec(memory_space=pltpu.SMEM), hbm, hbm, hbm],
        out_specs=pl.BlockSpec(memory_space=pltpu.VMEM),
        scratch_shapes=[V((1, 2, 256, 128), jnp.bfloat16), V((1, 2, 256, 128), jnp.bfloat16), V((2, 256, 256), F32), V((1, 256, 256), F32)]
        + [V(s, F32) for s in LAND + PIECES]
        + [pltpu.SemaphoreType.DMA((21,)), pltpu.SemaphoreType.DMA((21,)), pltpu.SemaphoreType.DMA((3,))],
        compiler_params=pltpu.CompilerParams(collective_id=0, has_side_effects=True, vmem_limit_bytes=60 << 20),
    )(ranks, diag, left, right)


def solution(mesh):
    in_specs = (P("row", None, None), P("row", "col", None, None), P("row", "col", None, None), P())
    return jax.shard_map(shards, mesh=mesh, in_specs=in_specs, out_specs=P("row", "col", None, None), check_vma=False)
```
